512 devices in a mesh: ctx: 64 (over y_hi, z, core), head: 8 (over y_lo, x).
Axes of the slice: x: 4, y: 4 (y_hi: 2, y_lo: 2; y = y_hi * 2 + y_lo), z: 16, core: 2. Of those that a mesh axis runs over, the one named last changes fastest.
Arguments:
- queries: bfloat16 [16384, 2048], P(('ctx', 'head')), may hold values from -16 to 16
- keys: bfloat16 [16384, 2048], P(('ctx', 'head')), may hold values from -16 to 16
- values: bfloat16 [16384, 2048], P(('ctx', 'head')), may hold values from -6 to 6
- d_attn: bfloat16 [16384, 2048], P(('ctx', 'head')), may hold values from -12 to 12
- fisher_key_prior: float32 [16384, 2048], P(('ctx', 'head')), may hold values from 0.05 to 0.5
- fisher_value_prior: float32 [16384, 2048], P(('ctx', 'head')), may hold values from 0.05 to 0.5
- doc_lengths: int32 [32], replicated, may hold values from 1 to 1024, 16384 in all
Outputs:
- grad_queries: bfloat16 [16384, 2048], P(('ctx', 'head'))
- grad_keys: bfloat16 [16384, 2048], P(('ctx', 'head'))
- grad_values: bfloat16 [16384, 2048], P(('ctx', 'head'))
- fisher_key: float32 [16384, 2048], P(('ctx', 'head'))
- fisher_value: float32 [16384, 2048], P(('ctx', 'head'))
The draws below stay inside these ranges and needn't reach their ends.
Inputs may be any that keep to these rules, and one draw needn't show every extreme that they name: `doc_lengths`: they sum to 16384; the longest has exactly 1024 tokens.
All inputs are finite; a program needn't handle non-finite values.
Results may differ from the reference program's by a relative error of at most 0.019.
Values may be sent and summed in bfloat16 or wider, within the bound.
No kernel may reach another device: no remote copies, remote signals or barrier semaphores. Data moves between devices by JAX's collectives and lax.ppermute only.
A program may use at most 64 MiB of HBM per device.

```python
import math
import jax
import jax.numpy as jnp
import numpy as np
from jax import lax

HD = 128
HEADS = 16
TOK_DEV = 256
BLOCK = 128
TOKENS = 16384
REACH = 8
MOST_DOC = 1024
NDOC = 32
N_CTX = 64


def draw_queries(key, part):
    key = jax.random.fold_in(key, 1)
    result = jnp.clip(jax.random.normal(key, (TOKENS, HEADS * HD), jnp.float32), -4.0, 4.0)
    return result.astype(jnp.bfloat16)


def draw_keys(key, part):
    key = jax.random.fold_in(key, 2)
    result = jnp.clip(jax.random.normal(key, (TOKENS, HEADS * HD), jnp.float32), -4.0, 4.0)
    return result.astype(jnp.bfloat16)


def block_levels(own_key, dims, shards, low, top_value):
    factor_of = 1.0
    for position, shards_of in shards:
        steps = jax.random.uniform(jax.random.fold_in(jax.random.fold_in(own_key, 6), position), (shards_of,), jnp.float32, low / len(shards), top_value / len(shards))
        factor_of = factor_of * jnp.repeat(jnp.exp(steps), dims[position] // shards_of).reshape((-1,) + (1,) * (len(dims) - 1 - position))
    return factor_of


def length_profile(amount, total, limit, slope):
    weights = [(1 << 20) // math.isqrt(grade ** slope) + 1 for grade in range(2, amount + 1)]
    spare, counts = total - limit - (amount - 1), [1] * (amount - 1)
    while spare > 0:
        movable = [i for i in range(amount - 1) if counts[i] < limit]
        mass, left = sum([weights[i] for i in movable]), spare
        for i in movable:
            addition = min(limit - counts[i], max(1, left * weights[i] // mass), spare)
            counts[i] = counts[i] + addition
            spare = spare - addition
    return np.array([limit] + counts)


def ragged(key, number_of, total, reach, slope):
    if number_of == 2:
        one = jax.random.randint(key, (), max(1, total - reach), min(reach, total - 1) + 1)
        return jnp.stack([one, total - one])
    lengths = jnp.asarray(length_profile(number_of, total, reach, slope), jnp.int32)
    couples = (number_of - 1) // 2
    donor, receiver = lengths[1:1 + 2 * couples:2], lengths[2:2 + 2 * couples:2]
    slack = jnp.minimum(donor - 1, reach - receiver)
    passed = jax.random.randint(jax.random.fold_in(key, 1), (couples,), 0, 1 << 20) % (slack + 1)
    lengths = lengths.at[1:1 + 2 * couples:2].set(donor - passed).at[2:2 + 2 * couples:2].set(receiver + passed)
    return lengths[jax.random.permutation(jax.random.fold_in(key, 2), number_of)]


def normal_values(own_key, extent, spread, limit, cuts=(), held_as=jnp.bfloat16):
    values = jax.random.normal(own_key, extent, jnp.float32) * spread
    if len(cuts) > 0:
        values = block_levels(own_key, extent, cuts, -0.22, 0.18) * values
    return jnp.clip(values, min=-limit, max=limit).astype(held_as)


def setup_inputs(seed: int = 0) -> dict:
    seeds = jax.random.split(jax.random.key(seed), 8)
    return {
        "queries": draw_queries(jax.random.fold_in(seeds[7], 71), 0),
        "keys": draw_keys(jax.random.fold_in(seeds[7], 71), 0),
        "values": normal_values(seeds[2], (TOKENS, HEADS * HD), 1.0, 6.0, ((0, 512),)),
        "d_attn": normal_values(seeds[3], (TOKENS, HEADS * HD), 2.0, 12.0, ((0, 512),)),
        "fisher_key_prior": jnp.clip(jnp.exp(math.log(0.5) - 2.3025851 * jax.random.uniform(seeds[4], (TOKENS, HEADS * HD), jnp.float32) ** block_levels(seeds[4], (TOKENS, HEADS * HD), ((0, 512),), -0.2, 0.2)), 0.05, 0.5),
        "fisher_value_prior": jnp.clip(jnp.exp(math.log(0.5) - 2.3025851 * jax.random.uniform(seeds[5], (TOKENS, HEADS * HD), jnp.float32) ** block_levels(seeds[5], (TOKENS, HEADS * HD), ((0, 512),), -0.2, 0.2)), 0.05, 0.5),
        "doc_lengths": ragged(seeds[6], NDOC, TOKENS, MOST_DOC, 2).astype(jnp.int32),
    }


def layout():
    seq_index = jnp.arange(TOKENS, dtype=jnp.int32)
    block_index = seq_index // BLOCK
    first_half = block_index < N_CTX
    holder = jnp.where(first_half, block_index, 2 * N_CTX - 1 - block_index)
    stored = holder * TOK_DEV + jnp.where(first_half, 0, BLOCK) + seq_index % BLOCK
    owner_dev = seq_index // TOK_DEV
    inner_row = seq_index % TOK_DEV
    seq_place = jnp.where(inner_row < BLOCK, owner_dev * BLOCK + inner_row, (2 * N_CTX - 1 - owner_dev) * BLOCK + inner_row - BLOCK)
    return (stored.astype(jnp.int32), seq_place.astype(jnp.int32))

def settle(array):
    return lax.optimization_barrier(array.astype(jnp.bfloat16)).astype(jnp.float32)

def reference(queries, keys, values, d_attn, fisher_key_prior, fisher_value_prior, doc_lengths):
    score_scale = 1.0 / math.sqrt(HD)
    stored, seq_place = layout()
    bounds = jnp.cumsum(doc_lengths).astype(jnp.int32)
    seq_index = jnp.arange(TOKENS, dtype=jnp.int32)
    doc_ids = lax.optimization_barrier(jnp.sum((seq_index[:, None] >= bounds[None, :]).astype(jnp.int32), axis=1)).astype(jnp.int32)

    def to_heads(array):
        return array[stored].reshape(TOKENS, HEADS, HD)
    q_seq = to_heads(queries)
    k_seq = to_heads(keys)
    v_seq = to_heads(values)
    d_seq = to_heads(d_attn)
    pad_len = REACH * BLOCK
    window = (REACH + 1) * BLOCK
    pad_rows = jnp.zeros((pad_len, HEADS, HD), jnp.bfloat16)
    pad_docs = jnp.full((pad_len,), -1, jnp.int32)
    k_front = jnp.concatenate([pad_rows, k_seq], axis=0)
    v_front = jnp.concatenate([pad_rows, v_seq], axis=0)
    docs_front = jnp.concatenate([pad_docs, doc_ids], axis=0)
    local_index = jnp.arange(BLOCK, dtype=jnp.int32)
    window_idx = jnp.arange(window, dtype=jnp.int32)

    def query_block(block_id):
        first_row = (block_id * BLOCK).astype(jnp.int32)
        q_rows = lax.dynamic_slice_in_dim(q_seq, first_row, BLOCK, 0).astype(jnp.float32)
        d_rows = lax.dynamic_slice_in_dim(d_seq, first_row, BLOCK, 0).astype(jnp.float32)
        k_rows = lax.dynamic_slice_in_dim(k_front, first_row, window, 0).astype(jnp.float32)
        v_rows = lax.dynamic_slice_in_dim(v_front, first_row, window, 0).astype(jnp.float32)
        q_docs = lax.dynamic_slice_in_dim(doc_ids, first_row, BLOCK, 0)
        k_docs = lax.dynamic_slice_in_dim(docs_front, first_row, window, 0)
        allowed = (q_docs[:, None] == k_docs[None, :]) & (window_idx[None, :] - pad_len <= local_index[:, None])
        scores = jnp.einsum('qhd,khd->hqk', q_rows, k_rows) * score_scale
        top_score = lax.optimization_barrier(jnp.max(jnp.where(allowed[None], scores, -jnp.inf), axis=2))
        running_sum = lax.optimization_barrier(jnp.sum(jnp.where(allowed[None], jnp.exp(scores - top_score[:, :, None]), 0.0), axis=2))
        log_total = top_score + jnp.log(running_sum)
        weights = jnp.where(allowed[None], jnp.exp(scores - log_total[:, :, None]), 0.0)
        attended = jnp.einsum('hqk,khd->qhd', settle(weights), v_rows)
        row_delta = lax.optimization_barrier(jnp.sum(d_rows * attended, axis=2)).T
        d_weights = jnp.einsum('qhd,khd->hqk', d_rows, v_rows)
        d_scores = settle(weights * (d_weights - row_delta[:, :, None]))
        grad_q = jnp.einsum('hqk,khd->qhd', d_scores, k_rows) * score_scale
        return (grad_q.astype(jnp.bfloat16), log_total, row_delta)
    grad_blocks, log_blocks, delta_blocks = lax.map(query_block, jnp.arange(2 * N_CTX, dtype=jnp.int32))
    log_seq = jnp.transpose(log_blocks, (1, 0, 2)).reshape(HEADS, TOKENS)
    delta_seq = jnp.transpose(delta_blocks, (1, 0, 2)).reshape(HEADS, TOKENS)
    q_back = jnp.concatenate([q_seq, pad_rows], axis=0)
    d_back = jnp.concatenate([d_seq, pad_rows], axis=0)
    docs_back = jnp.concatenate([doc_ids, pad_docs], axis=0)
    pad_stats = jnp.zeros((HEADS, pad_len), jnp.float32)
    log_back = jnp.concatenate([log_seq, pad_stats], axis=1)
    delta_back = jnp.concatenate([delta_seq, pad_stats], axis=1)

    def key_block(block_id):
        first_row = (block_id * BLOCK).astype(jnp.int32)
        k_rows = lax.dynamic_slice_in_dim(k_seq, first_row, BLOCK, 0).astype(jnp.float32)
        v_rows = lax.dynamic_slice_in_dim(v_seq, first_row, BLOCK, 0).astype(jnp.float32)
        q_rows = lax.dynamic_slice_in_dim(q_back, first_row, window, 0).astype(jnp.float32)
        d_rows = lax.dynamic_slice_in_dim(d_back, first_row, window, 0).astype(jnp.float32)
        k_docs = lax.dynamic_slice_in_dim(doc_ids, first_row, BLOCK, 0)
        q_docs = lax.dynamic_slice_in_dim(docs_back, first_row, window, 0)
        log_window = lax.dynamic_slice_in_dim(log_back, first_row, window, 1)
        delta_window = lax.dynamic_slice_in_dim(delta_back, first_row, window, 1)
        allowed = (q_docs[:, None] == k_docs[None, :]) & (local_index[None, :] <= window_idx[:, None])
        scores = jnp.einsum('qhd,khd->hqk', q_rows, k_rows) * score_scale
        weights = jnp.where(allowed[None], jnp.exp(scores - log_window[:, :, None]), 0.0)
        d_weights = jnp.einsum('qhd,khd->hqk', d_rows, v_rows)
        d_scores = settle(weights * (d_weights - delta_window[:, :, None]))
        grad_k = jnp.einsum('hqk,qhd->khd', d_scores, q_rows) * score_scale
        grad_v = jnp.einsum('hqk,qhd->khd', settle(weights), d_rows)
        return (grad_k.astype(jnp.bfloat16), grad_v.astype(jnp.bfloat16))
    key_grad_blocks, value_grad_blocks = lax.map(key_block, jnp.arange(2 * N_CTX, dtype=jnp.int32))
    grad_queries = grad_blocks.reshape(TOKENS, HEADS * HD)[seq_place]
    grad_keys = key_grad_blocks.reshape(TOKENS, HEADS * HD)[seq_place]
    grad_values = value_grad_blocks.reshape(TOKENS, HEADS * HD)[seq_place]
    key_wide = grad_keys.astype(jnp.float32)
    value_wide = grad_values.astype(jnp.float32)
    fisher_key = fisher_key_prior + key_wide * key_wide
    fisher_value = fisher_value_prior + value_wide * value_wide
    return (grad_queries, grad_keys, grad_values, fisher_key, fisher_value)
```

```python
import jax
import jax.numpy as jnp
from jax import lax
from jax.experimental import pallas as pl
from jax.experimental.pallas import tpu as pltpu
from jax.sharding import PartitionSpec as P

HD = 128
HEADS = 16
ROWS = 32
SEG = 512
SEGS = 32
NDOC = 32
TOKENS = SEG * SEGS
WIN = 2 * SEG
QB = 256
KB = 128
SCALE = 1.0 / HD**0.5
LOG2E = 1.4426950408889634
AXES = ("ctx", "head")
MASKED = -1e30


def device_of(segment, slot):
    column = slot % 4
    if segment < SEGS // 2:
        return (4 * segment + slot // 4) * 8 + column
    return (4 * (SEGS - 1 - segment) + 3 - slot // 4) * 8 + 4 + column


GROUPS = [[device_of(s, i) for i in range(16)] for s in range(SEGS)]
TO_NEXT = [(device_of(s, i), device_of((s + 1) % SEGS, i)) for s in range(SEGS) for i in range(16)]
TO_PREV = [(target, source) for source, target in TO_NEXT]


def to_next(block):
    return lax.ppermute(block, AXES, TO_NEXT)


def to_prev(block):
    return lax.ppermute(block, AXES, TO_PREV)


def exchange(chunks):
    return lax.all_to_all(
        chunks, AXES, split_axis=0, concat_axis=0, axis_index_groups=GROUPS, tiled=True
    )


def place():
    ctx = lax.axis_index("ctx")
    head = lax.axis_index("head")
    lower = head < 4
    segment = jnp.where(lower, ctx // 4, SEGS - 1 - ctx // 4)
    slot = jnp.where(lower, ctx % 4, 3 - ctx % 4) * 4 + head % 4
    return segment.astype(jnp.int32), slot.astype(jnp.int32)


def doc_table(lengths_ref):
    table = []
    first = jnp.int32(0)
    for doc in range(NDOC):
        end = first + lengths_ref[doc]
        middle = lax.shift_right_logical(first + end, 1)
        table.append((first, end, lax.shift_right_logical(middle, 9)))
        first = end
    return table


def halo_split(table, segment):
    split = jnp.int32(0)
    for first, end, owner in table:
        split = jnp.maximum(split, jnp.where(owner == segment, end - (segment + 1) * SEG, 0))
    return split


def own_split(table, segment):
    head_end = jnp.int32(0)
    tail_start = jnp.int32(SEG)
    for first, end, owner in table:
        head_end = jnp.maximum(head_end, jnp.where(owner == segment - 1, end - segment * SEG, 0))
        tail_start = jnp.minimum(
            tail_start, jnp.where(owner == segment + 1, first - segment * SEG, SEG)
        )
    return head_end, tail_start


def pick(condition, left, right):
    chosen = jnp.where(condition, left.astype(jnp.float32), right.astype(jnp.float32))
    return chosen.astype(jnp.bfloat16)


def pack_kernel(q_ref, d_ref, k_ref, v_ref, rows_ref, chunk_ref):
    rows_ref[0:ROWS, :] = q_ref[...]
    rows_ref[ROWS : 2 * ROWS, :] = d_ref[...]
    for h in range(HEADS):
        chunk_ref[h, 0:ROWS, :] = k_ref[:, h * HD : (h + 1) * HD]
        chunk_ref[h, ROWS : 2 * ROWS, :] = v_ref[:, h * HD : (h + 1) * HD]


def halo_kernel(lengths_ref, q_ref, d_ref, before_ref, after_ref, chunk_ref):
    segment, slot = place()
    split = halo_split(doc_table(lengths_ref), segment)
    row = slot * ROWS + lax.broadcasted_iota(jnp.int32, (ROWS, HD), 0)
    after = row < split
    for h in range(HEADS):
        cols = slice(h * HD, (h + 1) * HD)
        chunk_ref[h, 0:ROWS, :] = q_ref[:, cols]
        chunk_ref[h, ROWS : 2 * ROWS, :] = d_ref[:, cols]
        for part in range(2):
            rows = slice(part * ROWS, (part + 1) * ROWS)
            chunk_ref[h, (2 + part) * ROWS : (3 + part) * ROWS, :] = pick(
                after, after_ref[rows, cols], before_ref[rows, cols]
            )


def attention_kernel(
    lengths_ref,
    own_ref,
    before_ref,
    after_ref,
    qd_ref,
    halo_out,
    own_out,
    dq_out,
    q_win,
    d_win,
    k_win,
    v_win,
    s_buf,
    dp_buf,
    dk_acc,
    dv_acc,
):
    segment, unused_slot = place()
    table = doc_table(lengths_ref)
    split = halo_split(table, segment)
    tile_row = lax.broadcasted_iota(jnp.int32, (ROWS, HD), 0)
    for i in range(16):
        halo = slice(i * ROWS, (i + 1) * ROWS)
        mine = slice(SEG + i * ROWS, SEG + (i + 1) * ROWS)
        after = tile_row + i * ROWS < split
        k_win[halo, :] = pick(after, after_ref[i, 0:ROWS, :], before_ref[i, 0:ROWS, :])
        v_win[halo, :] = pick(
            after, after_ref[i, ROWS : 2 * ROWS, :], before_ref[i, ROWS : 2 * ROWS, :]
        )
        k_win[mine, :] = own_ref[i, 0:ROWS, :]
        v_win[mine, :] = own_ref[i, ROWS : 2 * ROWS, :]
        q_win[mine, :] = qd_ref[i, 0:ROWS, :]
        d_win[mine, :] = qd_ref[i, ROWS : 2 * ROWS, :]
        q_win[halo, :] = qd_ref[i, 2 * ROWS : 3 * ROWS, :]
        d_win[halo, :] = qd_ref[i, 3 * ROWS : 4 * ROWS, :]
    base = (segment - 1) * SEG
    contract_last = (((1,), (1,)), ((), ()))
    contract_first = (((0,), (0,)), ((), ()))
    for qb in range(WIN // QB):
        index = qb * QB + lax.broadcasted_iota(jnp.int32, (1, QB), 1)
        q_pos = base + index + jnp.where(index < split, WIN, 0)
        q_first = jnp.full((1, QB), -TOKENS, jnp.int32)
        for first, unused_end, unused_owner in table:
            q_first = jnp.where(q_pos >= first, first, q_first)
        q_first = jnp.where(q_pos >= TOKENS, TOKENS, q_first)
        rows = slice(qb * QB, (qb + 1) * QB)
        q_rows = q_win[rows, :]
        d_rows = d_win[rows, :]
        top = jnp.full((8, QB), MASKED, jnp.float32)
        for kb in range(WIN // KB):
            keys = slice(kb * KB, (kb + 1) * KB)
            k_index = kb * KB + lax.broadcasted_iota(jnp.int32, (KB, QB), 0)
            k_pos = base + k_index
            if kb * KB < SEG:
                k_pos = k_pos + jnp.where(k_index < split, WIN, 0)
            allowed = (k_pos >= q_first) & (k_pos <= q_pos)
            scores = lax.dot_general(
                k_win[keys, :], q_rows, contract_last, preferred_element_type=jnp.float32
            )
            scores = jnp.where(allowed, scores, MASKED)
            s_buf[keys, :] = scores
            top = jnp.maximum(top, jnp.max(scores.reshape(KB // 8, 8, QB), axis=0))
        top = jnp.max(top, axis=0, keepdims=True)
        total = jnp.zeros((8, QB), jnp.float32)
        for kb in range(WIN // KB):
            keys = slice(kb * KB, (kb + 1) * KB)
            terms = jnp.exp2((s_buf[keys, :] - top) * (SCALE * LOG2E))
            s_buf[keys, :] = terms
            total = total + jnp.sum(terms.reshape(KB // 8, 8, QB), axis=0)
        inverse = 1.0 / jnp.sum(total, axis=0, keepdims=True)
        delta = jnp.zeros((8, QB), jnp.float32)
        for kb in range(WIN // KB):
            keys = slice(kb * KB, (kb + 1) * KB)
            probs = s_buf[keys, :] * inverse
            probs_b = probs.astype(jnp.bfloat16)
            d_probs = lax.dot_general(
                v_win[keys, :], d_rows, contract_last, preferred_element_type=jnp.float32
            )
            s_buf[keys, :] = probs
            dp_buf[keys, :] = d_probs
            delta = delta + jnp.sum(
                (probs_b.astype(jnp.float32) * d_probs).reshape(KB // 8, 8, QB), axis=0
            )
            part = jnp.dot(probs_b, d_rows, preferred_element_type=jnp.float32)
            dv_acc[keys, :] = part if qb == 0 else dv_acc[keys, :] + part
        delta = jnp.sum(delta, axis=0, keepdims=True)
        dq = jnp.zeros((QB, HD), jnp.float32)
        for kb in range(WIN // KB):
            keys = slice(kb * KB, (kb + 1) * KB)
            d_scores = (s_buf[keys, :] * (dp_buf[keys, :] - delta)).astype(jnp.bfloat16)
            part = jnp.dot(d_scores, q_rows, preferred_element_type=jnp.float32)
            dk_acc[keys, :] = part if qb == 0 else dk_acc[keys, :] + part
            dq = dq + lax.dot_general(
                d_scores, k_win[keys, :], contract_first, preferred_element_type=jnp.float32
            )
        dq = (dq * SCALE).astype(jnp.bfloat16)
        for i in range(QB // ROWS):
            index = qb * (QB // ROWS) + i
            place_row = (1 - index // 16) * ROWS
            dq_out[index % 16, place_row : place_row + ROWS, :] = dq[i * ROWS : (i + 1) * ROWS, :]
    halo_out[0:SEG, :] = (dk_acc[0:SEG, :] * SCALE).astype(jnp.bfloat16)
    halo_out[SEG:WIN, :] = dv_acc[0:SEG, :].astype(jnp.bfloat16)
    own_out[0:SEG, :] = (dk_acc[SEG:WIN, :] * SCALE).astype(jnp.bfloat16)
    own_out[SEG:WIN, :] = dv_acc[SEG:WIN, :].astype(jnp.bfloat16)


def merge_kernel(lengths_ref, own_ref, before_ref, after_ref, chunk_ref):
    segment, unused_slot = place()
    head_end, tail_start = own_split(doc_table(lengths_ref), segment)
    tile_row = lax.broadcasted_iota(jnp.int32, (ROWS, HD), 0)
    for i in range(16):
        row = tile_row + i * ROWS
        for part in range(2):
            rows = slice(part * SEG + i * ROWS, part * SEG + (i + 1) * ROWS)
            chosen = jnp.where(
                row >= tail_start,
                after_ref[rows, :].astype(jnp.float32),
                own_ref[rows, :].astype(jnp.float32),
            )
            chosen = jnp.where(row < head_end, before_ref[rows, :].astype(jnp.float32), chosen)
            chunk_ref[i, part * ROWS : (part + 1) * ROWS, :] = chosen.astype(jnp.bfloat16)


def finish_kernel(
    lengths_ref,
    kv_ref,
    dq_ref,
    before_ref,
    after_ref,
    key_prior_ref,
    value_prior_ref,
    dq_out,
    dk_out,
    dv_out,
    key_out,
    value_out,
):
    segment, slot = place()
    head_end, tail_start = own_split(doc_table(lengths_ref), segment)
    row = slot * ROWS + lax.broadcasted_iota(jnp.int32, (ROWS, HD), 0)
    from_after = row >= tail_start
    from_before = row < head_end
    for h in range(HEADS):
        cols = slice(h * HD, (h + 1) * HD)
        chosen = jnp.where(
            from_after,
            after_ref[h].astype(jnp.float32),
            dq_ref[h, 0:ROWS, :].astype(jnp.float32),
        )
        chosen = jnp.where(from_before, before_ref[h].astype(jnp.float32), chosen)
        dq_out[:, cols] = chosen.astype(jnp.bfloat16)
        dk = kv_ref[h, 0:ROWS, :]
        dv = kv_ref[h, ROWS : 2 * ROWS, :]
        dk_out[:, cols] = dk
        dv_out[:, cols] = dv
        dk = dk.astype(jnp.float32)
        dv = dv.astype(jnp.float32)
        key_out[:, cols] = key_prior_ref[:, cols] + dk * dk
        value_out[:, cols] = value_prior_ref[:, cols] + dv * dv


SMEM = pl.BlockSpec(memory_space=pltpu.SMEM)
VMEM = pl.BlockSpec(memory_space=pltpu.VMEM)


def bf16(*shape):
    return jax.ShapeDtypeStruct(shape, jnp.bfloat16)


def call(kernel, inputs, outputs, scratch=(), smem=1, limit=16 << 20):
    return pl.pallas_call(
        kernel,
        in_specs=[SMEM] * smem + [VMEM] * (len(inputs) - smem),
        out_specs=[VMEM] * len(outputs),
        out_shape=list(outputs),
        scratch_shapes=list(scratch),
        compiler_params=pltpu.CompilerParams(vmem_limit_bytes=limit),
        name=kernel.__name__,
    )(*inputs)


def shards(queries, keys, values, d_attn, fisher_key_prior, fisher_value_prior, doc_lengths):
    width = HEADS * HD
    qd_rows, kv_chunks = call(
        pack_kernel,
        (queries, d_attn, keys, values),
        (bf16(2 * ROWS, width), bf16(HEADS, 2 * ROWS, HD)),
        smem=0,
    )
    qd_before = to_next(qd_rows)
    qd_after = to_prev(qd_rows)
    kv_own = exchange(kv_chunks)
    kv_before = to_next(kv_own)
    kv_after = to_prev(kv_own)
    (qd_chunks,) = call(
        halo_kernel,
        (doc_lengths, queries, d_attn, qd_before, qd_after),
        (bf16(HEADS, 4 * ROWS, HD),),
    )
    qd_heads = exchange(qd_chunks)
    window = [pltpu.VMEM((WIN, HD), jnp.bfloat16)] * 4
    halo_kv, own_kv, dq_chunks = call(
        attention_kernel,
        (doc_lengths, kv_own, kv_before, kv_after, qd_heads),
        (bf16(WIN, HD), bf16(WIN, HD), bf16(16, 2 * ROWS, HD)),
        scratch=window
        + [pltpu.VMEM((WIN, QB), jnp.float32)] * 2
        + [pltpu.VMEM((WIN, HD), jnp.float32)] * 2,
        limit=32 << 20,
    )
    halo_before = to_next(halo_kv)
    halo_after = to_prev(halo_kv)
    dq_heads = exchange(dq_chunks)
    dq_halo = dq_heads[:, ROWS:, :]
    dq_before = to_next(dq_halo)
    dq_after = to_prev(dq_halo)
    (kv_back,) = call(
        merge_kernel,
        (doc_lengths, own_kv, halo_before, halo_after),
        (bf16(16, 2 * ROWS, HD),),
    )
    kv_heads = exchange(kv_back)
    wide = jax.ShapeDtypeStruct((ROWS, width), jnp.float32)
    return call(
        finish_kernel,
        (doc_lengths, kv_heads, dq_heads, dq_before, dq_after, fisher_key_prior, fisher_value_prior),
        (bf16(ROWS, width), bf16(ROWS, width), bf16(ROWS, width), wide, wide),
    )


def solution(mesh):
    tokens = P(AXES, None)
    return jax.shard_map(
        shards,
        mesh=mesh,
        in_specs=(tokens,) * 6 + (P(),),
        out_specs=(tokens,) * 5,
        check_vma=False,
    )
```

```python
import jax
import jax.numpy as jnp
from jax import lax
from jax.experimental import pallas as pl
from jax.experimental.pallas import tpu as pltpu
from jax.sharding import PartitionSpec as P

HD = 128
HEADS = 16
ROWS = 32
SEG = 512
SEGS = 32
NDOC = 32
TOKENS = SEG * SEGS
WIN = 2 * SEG
QB = 256
KB = 128
SCALE = 1.0 / HD**0.5
LOG2E = 1.4426950408889634
AXES = ("ctx", "head")
MASKED = -1e30


def device_of(segment, slot):
    column = slot % 4
    if segment < SEGS // 2:
        return (4 * segment + slot // 4) * 8 + column
    return (4 * (SEGS - 1 - segment) + 3 - slot // 4) * 8 + 4 + column


GROUPS = [[device_of(s, i) for i in range(16)] for s in range(SEGS)]
def swaps(first):
    pairs = []
    for s in range(first, SEGS - 1, 2):
        for i in range(16):
            here, there = device_of(s, i), device_of(s + 1, i)
            pairs += [(here, there), (there, here)]
    return pairs


EVEN = swaps(0)
ODD = swaps(1)


def with_even(block):
    return lax.ppermute(block, AXES, EVEN)


def with_odd(block):
    return lax.ppermute(block, AXES, ODD)


def exchange(chunks):
    return lax.all_to_all(
        chunks, AXES, split_axis=0, concat_axis=0, axis_index_groups=GROUPS, tiled=True
    )


def place():
    ctx = lax.axis_index("ctx")
    head = lax.axis_index("head")
    lower = head < 4
    segment = jnp.where(lower, ctx // 4, SEGS - 1 - ctx // 4)
    slot = jnp.where(lower, ctx % 4, 3 - ctx % 4) * 4 + head % 4
    return segment.astype(jnp.int32), slot.astype(jnp.int32)


def doc_table(lengths_ref):
    table = []
    first = jnp.int32(0)
    for doc in range(NDOC):
        end = first + lengths_ref[doc]
        middle = lax.shift_right_logical(first + end, 1)
        table.append((first, end, lax.shift_right_logical(middle, 9)))
        first = end
    return table


def halo_split(table, segment):
    split = jnp.int32(0)
    for first, end, owner in table:
        split = jnp.maximum(split, jnp.where(owner == segment, end - (segment + 1) * SEG, 0))
    return split


def own_split(table, segment):
    head_end = jnp.int32(0)
    tail_start = jnp.int32(SEG)
    for first, end, owner in table:
        head_end = jnp.maximum(head_end, jnp.where(owner == segment - 1, end - segment * SEG, 0))
        tail_start = jnp.minimum(
            tail_start, jnp.where(owner == segment + 1, first - segment * SEG, SEG)
        )
    return head_end, tail_start


def pick(condition, left, right):
    chosen = jnp.where(condition, left.astype(jnp.float32), right.astype(jnp.float32))
    return chosen.astype(jnp.bfloat16)


def pack_kernel(q_hbm, k_hbm, v_hbm, d_hbm, chunk_ref, rows, sems):
    copies = [
        pltpu.make_async_copy(source, rows.at[part], sems.at[part])
        for part, source in enumerate((q_hbm, k_hbm, v_hbm, d_hbm))
    ]
    for copy in copies:
        copy.start()
    for part, copy in enumerate(copies):
        copy.wait()
        for h in range(HEADS):
            chunk_ref[h, part * ROWS : (part + 1) * ROWS, :] = rows[
                part, :, h * HD : (h + 1) * HD
            ]


def attention_kernel(
    lengths_ref,
    own_ref,
    even_ref,
    odd_ref,
    own_out,
    halo_out,
    q_win,
    k_win,
    v_win,
    d_win,
    s_buf,
    dp_buf,
    dk_acc,
    dv_acc,
):
    segment, unused_slot = place()
    table = doc_table(lengths_ref)
    split = halo_split(table, segment)
    tile_row = lax.broadcasted_iota(jnp.int32, (ROWS, HD), 0)
    odd = segment % 2 == 1
    for i in range(16):
        halo = slice(i * ROWS, (i + 1) * ROWS)
        mine = slice(SEG + i * ROWS, SEG + (i + 1) * ROWS)
        from_even = (tile_row + i * ROWS < split) != odd
        for part, win in enumerate((q_win, k_win, v_win, d_win)):
            rows = slice(part * ROWS, (part + 1) * ROWS)
            win[halo, :] = pick(from_even, even_ref[i, rows, :], odd_ref[i, rows, :])
            win[mine, :] = own_ref[i, rows, :]
    base = (segment - 1) * SEG
    contract_last = (((1,), (1,)), ((), ()))
    contract_first = (((0,), (0,)), ((), ()))
    for qb in range(WIN // QB):
        index = qb * QB + lax.broadcasted_iota(jnp.int32, (1, QB), 1)
        q_pos = base + index + jnp.where(index < split, WIN, 0)
        q_first = jnp.full((1, QB), -TOKENS, jnp.int32)
        for first, unused_end, unused_owner in table:
            q_first = jnp.where(q_pos >= first, first, q_first)
        q_first = jnp.where(q_pos >= TOKENS, TOKENS, q_first)
        rows = slice(qb * QB, (qb + 1) * QB)
        q_rows = q_win[rows, :]
        d_rows = d_win[rows, :]
        top = jnp.full((8, QB), MASKED, jnp.float32)
        for kb in range(WIN // KB):
            keys = slice(kb * KB, (kb + 1) * KB)
            k_index = kb * KB + lax.broadcasted_iota(jnp.int32, (KB, QB), 0)
            k_pos = base + k_index
            if kb * KB < SEG:
                k_pos = k_pos + jnp.where(k_index < split, WIN, 0)
            allowed = (k_pos >= q_first) & (k_pos <= q_pos)
            scores = lax.dot_general(
                k_win[keys, :], q_rows, contract_last, preferred_element_type=jnp.float32
            )
            scores = jnp.where(allowed, scores, MASKED)
            s_buf[keys, :] = scores
            top = jnp.maximum(top, jnp.max(scores.reshape(KB // 8, 8, QB), axis=0))
        top = jnp.max(top, axis=0, keepdims=True)
        total = jnp.zeros((8, QB), jnp.float32)
        for kb in range(WIN // KB):
            keys = slice(kb * KB, (kb + 1) * KB)
            terms = jnp.exp2((s_buf[keys, :] - top) * (SCALE * LOG2E))
            s_buf[keys, :] = terms
            total = total + jnp.sum(terms.reshape(KB // 8, 8, QB), axis=0)
        inverse = 1.0 / jnp.sum(total, axis=0, keepdims=True)
        delta = jnp.zeros((8, QB), jnp.float32)
        for kb in range(WIN // KB):
            keys = slice(kb * KB, (kb + 1) * KB)
            probs = s_buf[keys, :] * inverse
            probs_b = probs.astype(jnp.bfloat16)
            d_probs = lax.dot_general(
                v_win[keys, :], d_rows, contract_last, preferred_element_type=jnp.float32
            )
            s_buf[keys, :] = probs
            dp_buf[keys, :] = d_probs
            delta = delta + jnp.sum(
                (probs_b.astype(jnp.float32) * d_probs).reshape(KB // 8, 8, QB), axis=0
            )
            part = jnp.dot(probs_b, d_rows, preferred_element_type=jnp.float32)
            dv_acc[keys, :] = part if qb == 0 else dv_acc[keys, :] + part
        delta = jnp.sum(delta, axis=0, keepdims=True)
        dq = jnp.zeros((QB, HD), jnp.float32)
        for kb in range(WIN // KB):
            keys = slice(kb * KB, (kb + 1) * KB)
            d_scores = (s_buf[keys, :] * (dp_buf[keys, :] - delta)).astype(jnp.bfloat16)
            part = jnp.dot(d_scores, q_rows, preferred_element_type=jnp.float32)
            dk_acc[keys, :] = part if qb == 0 else dk_acc[keys, :] + part
            dq = dq + lax.dot_general(
                d_scores, k_win[keys, :], contract_first, preferred_element_type=jnp.float32
            )
        dq = (dq * SCALE).astype(jnp.bfloat16)
        for i in range(QB // ROWS):
            index = qb * (QB // ROWS) + i
            target = halo_out if index < 16 else own_out
            target[index % 16, 0:ROWS, :] = dq[i * ROWS : (i + 1) * ROWS, :]
    for i in range(16):
        halo = slice(i * ROWS, (i + 1) * ROWS)
        mine = slice(SEG + i * ROWS, SEG + (i + 1) * ROWS)
        for target, rows in ((halo_out, halo), (own_out, mine)):
            target[i, ROWS : 2 * ROWS, :] = (dk_acc[rows, :] * SCALE).astype(jnp.bfloat16)
            target[i, 2 * ROWS : 3 * ROWS, :] = dv_acc[rows, :].astype(jnp.bfloat16)


def merge_kernel(lengths_ref, own_ref, even_ref, odd_ref, chunk_ref):
    segment, unused_slot = place()
    head_end, tail_start = own_split(doc_table(lengths_ref), segment)
    odd = segment % 2 == 1
    tile_row = lax.broadcasted_iota(jnp.int32, (ROWS, HD), 0)
    for i in range(16):
        row = tile_row + i * ROWS
        before = row < head_end
        after = row >= tail_start
        from_even = (before & odd) | (after & jnp.logical_not(odd))
        from_own = jnp.logical_not(before | after)
        for part in range(3):
            rows = slice(part * ROWS, (part + 1) * ROWS)
            chosen = pick(from_even, even_ref[i, rows, :], odd_ref[i, rows, :])
            chunk_ref[i, rows, :] = pick(from_own, own_ref[i, rows, :], chosen)


def finish_kernel(
    back_ref,
    key_prior_ref,
    value_prior_ref,
    dq_out,
    dk_out,
    dv_out,
    key_out,
    value_out,
):
    for h in range(HEADS):
        cols = slice(h * HD, (h + 1) * HD)
        dq_out[:, cols] = back_ref[h, 0:ROWS, :]
        dk = back_ref[h, ROWS : 2 * ROWS, :]
        dv = back_ref[h, 2 * ROWS : 3 * ROWS, :]
        dk_out[:, cols] = dk
        dv_out[:, cols] = dv
        dk = dk.astype(jnp.float32)
        dv = dv.astype(jnp.float32)
        key_out[:, cols] = key_prior_ref[:, cols] + dk * dk
        value_out[:, cols] = value_prior_ref[:, cols] + dv * dv


SMEM = pl.BlockSpec(memory_space=pltpu.SMEM)
VMEM = pl.BlockSpec(memory_space=pltpu.VMEM)


def bf16(*shape):
    return jax.ShapeDtypeStruct(shape, jnp.bfloat16)


ANY = pl.BlockSpec(memory_space=pl.ANY)


def call(kernel, inputs, outputs, specs, scratch=(), limit=16 << 20):
    return pl.pallas_call(
        kernel,
        in_specs=specs,
        out_specs=[VMEM] * len(outputs),
        out_shape=list(outputs),
        scratch_shapes=list(scratch),
        compiler_params=pltpu.CompilerParams(vmem_limit_bytes=limit),
        name=kernel.__name__,
    )(*inputs)


def shards(queries, keys, values, d_attn, fisher_key_prior, fisher_value_prior, doc_lengths):
    width = HEADS * HD
    (chunks,) = call(
        pack_kernel,
        (queries, keys, values, d_attn),
        (bf16(HEADS, 4 * ROWS, HD),),
        [ANY] * 4,
        scratch=[pltpu.VMEM((4, ROWS, width), jnp.bfloat16), pltpu.SemaphoreType.DMA((4,))],
    )
    own = exchange(chunks)
    own_grads, halo_grads = call(
        attention_kernel,
        (doc_lengths, own, with_even(own), with_odd(own)),
        (bf16(16, 3 * ROWS, HD), bf16(16, 3 * ROWS, HD)),
        [SMEM] + [VMEM] * 3,
        scratch=[pltpu.VMEM((WIN, HD), jnp.bfloat16)] * 4
        + [pltpu.VMEM((WIN, QB), jnp.float32)] * 2
        + [pltpu.VMEM((WIN, HD), jnp.float32)] * 2,
        limit=32 << 20,
    )
    (merged,) = call(
        merge_kernel,
        (doc_lengths, own_grads, with_even(halo_grads), with_odd(halo_grads)),
        (bf16(16, 3 * ROWS, HD),),
        [SMEM] + [VMEM] * 3,
    )
    back = exchange(merged)
    wide = jax.ShapeDtypeStruct((ROWS, width), jnp.float32)
    return call(
        finish_kernel,
        (back, fisher_key_prior, fisher_value_prior),
        (bf16(ROWS, width), bf16(ROWS, width), bf16(ROWS, width), wide, wide),
        [VMEM] * 3,
    )


def solution(mesh):
    tokens = P(AXES, None)
    return jax.shard_map(
        shards,
        mesh=mesh,
        in_specs=(tokens,) * 6 + (P(),),
        out_specs=(tokens,) * 5,
        check_vma=False,
    )
```

```python
import jax
import jax.numpy as jnp
from jax import lax
from jax.experimental import pallas as pl
from jax.experimental.pallas import tpu as pltpu
from jax.sharding import PartitionSpec as P

HD = 128
HEADS = 16
ROWS = 32
SEG = 512
SEGS = 32
NDOC = 32
TOKENS = SEG * SEGS
WIN = 2 * SEG
QB = 256
KB = 128
SCALE = 1.0 / HD**0.5
LOG2E = 1.4426950408889634
EXPONENT = SCALE * LOG2E
AXES = ("ctx", "head")
MASKED = -1e30


def device_of(segment, slot):
    column = slot % 4
    if segment < SEGS // 2:
        return (4 * segment + slot // 4) * 8 + column
    return (4 * (SEGS - 1 - segment) + 3 - slot // 4) * 8 + 4 + column


GROUPS = [[device_of(s, i) for i in range(16)] for s in range(SEGS)]
UP = [(device_of(s, i), device_of(s + 1, i)) for s in range(SEGS - 1) for i in range(16)]
DOWN = [(target, source) for source, target in UP]


def to_after(block):
    return lax.ppermute(block, AXES, UP)


def to_before(block):
    return lax.ppermute(block, AXES, DOWN)


def exchange(chunks):
    return lax.all_to_all(
        chunks, AXES, split_axis=0, concat_axis=0, axis_index_groups=GROUPS, tiled=True
    )


def place():
    ctx = lax.axis_index("ctx")
    head = lax.axis_index("head")
    lower = head < 4
    segment = jnp.where(lower, ctx // 4, SEGS - 1 - ctx // 4)
    slot = jnp.where(lower, ctx % 4, 3 - ctx % 4) * 4 + head % 4
    return segment.astype(jnp.int32), slot.astype(jnp.int32)


def doc_bounds(lengths_ref):
    bounds = []
    first = jnp.int32(0)
    for doc in range(NDOC):
        bounds.append(first)
        first = first + lengths_ref[doc]
    return bounds


def rows_after(lengths_ref, segment):
    start = segment * SEG
    count = jnp.int32(0)
    first = jnp.int32(0)
    for doc in range(NDOC):
        end = first + lengths_ref[doc]
        count = jnp.maximum(count, jnp.where(first < start, end - start - SEG, 0))
        first = end
    return count


def first_positions(bounds, q_pos):
    q_first = jnp.zeros(q_pos.shape, jnp.int32)
    for first in bounds:
        q_first = jnp.where(q_pos >= first, first, q_first)
    return jnp.where(q_pos >= TOKENS, TOKENS, q_first)


def tiles_of(qb):
    return range(6) if qb == 0 else range(8) if qb == 1 else range(4)


def fill_windows(own_ref, before_ref, after_ref, k_win, v_win, q_win, d_win):
    for i in range(16):
        low = slice(i * ROWS, (i + 1) * ROWS)
        high = slice(SEG + i * ROWS, SEG + (i + 1) * ROWS)
        first = slice(0, ROWS)
        second = slice(ROWS, 2 * ROWS)
        k_win[low, :] = before_ref[i, first, :]
        v_win[low, :] = before_ref[i, second, :]
        k_win[high, :] = own_ref[i, first, :]
        v_win[high, :] = own_ref[i, second, :]
        q_win[low, :] = own_ref[i, 2 * ROWS : 3 * ROWS, :]
        d_win[low, :] = own_ref[i, 3 * ROWS : 4 * ROWS, :]
        q_win[high, :] = after_ref[i, first, :]
        d_win[high, :] = after_ref[i, second, :]


def tile_allowed(base, q_pos, q_first, qb, kb):
    k_pos = base + kb * KB + lax.broadcasted_iota(jnp.int32, (KB, QB), 0)
    allowed = k_pos >= q_first
    if kb >= 4 + 2 * qb:
        allowed = allowed & (k_pos <= q_pos)
    return allowed


CONTRACT_LAST = (((1,), (1,)), ((), ()))
CONTRACT_FIRST = (((0,), (0,)), ((), ()))


def dot_t(left, right):
    return lax.dot_general(left, right, CONTRACT_LAST, preferred_element_type=jnp.float32)


def pack_kernel(q_hbm, k_hbm, v_hbm, d_hbm, chunk_ref, rows, sems):
    copies = [
        pltpu.make_async_copy(source, rows.at[part], sems.at[part])
        for part, source in enumerate((k_hbm, v_hbm, q_hbm, d_hbm))
    ]
    for copy in copies:
        copy.start()
    for part, copy in enumerate(copies):
        copy.wait()
        for h in range(HEADS):
            chunk_ref[h, part * ROWS : (part + 1) * ROWS, :] = rows[
                part, :, h * HD : (h + 1) * HD
            ]


def split_kernel(own_ref, kv_ref, qd_ref):
    for i in range(16):
        kv_ref[i] = own_ref[i, 0 : 2 * ROWS, :]
        qd_ref[i] = own_ref[i, 2 * ROWS : 4 * ROWS, :]


def stats_kernel(
    lengths_ref,
    own_ref,
    before_ref,
    after_ref,
    own_stats,
    after_stats,
    k_win,
    v_win,
    q_win,
    d_win,
    s_buf,
):
    segment, unused_slot = place()
    fill_windows(own_ref, before_ref, after_ref, k_win, v_win, q_win, d_win)
    bounds = doc_bounds(lengths_ref)
    base = (segment - 1) * SEG

    def block(qb):
        q_pos = segment * SEG + qb * QB + lax.broadcasted_iota(jnp.int32, (1, QB), 1)
        q_first = first_positions(bounds, q_pos)
        q_rows = q_win[qb * QB : (qb + 1) * QB, :]
        d_rows = d_win[qb * QB : (qb + 1) * QB, :]
        top = jnp.full((8, QB), MASKED, jnp.float32)
        for kb in tiles_of(qb):
            keys = slice(kb * KB, (kb + 1) * KB)
            allowed = tile_allowed(base, q_pos, q_first, qb, kb)
            scores = jnp.where(allowed, dot_t(k_win[keys, :], q_rows), MASKED)
            s_buf[keys, :] = scores
            top = jnp.maximum(top, jnp.max(scores.reshape(KB // 8, 8, QB), axis=0))
        top = jnp.max(top, axis=0, keepdims=True)
        total = jnp.zeros((8, QB), jnp.float32)
        delta = jnp.zeros((8, QB), jnp.float32)
        for kb in tiles_of(qb):
            keys = slice(kb * KB, (kb + 1) * KB)
            terms = jnp.exp2((s_buf[keys, :] - top) * EXPONENT)
            s_buf[keys, :] = terms
            total = total + jnp.sum(terms.reshape(KB // 8, 8, QB), axis=0)
        total = jnp.sum(total, axis=0, keepdims=True)
        inverse = 1.0 / total
        for kb in tiles_of(qb):
            keys = slice(kb * KB, (kb + 1) * KB)
            probs_b = (s_buf[keys, :] * inverse).astype(jnp.bfloat16).astype(jnp.float32)
            weighted = probs_b * dot_t(v_win[keys, :], d_rows)
            delta = delta + jnp.sum(weighted.reshape(KB // 8, 8, QB), axis=0)
        target = own_stats if qb < 2 else after_stats
        cols = slice((qb % 2) * QB, (qb % 2 + 1) * QB)
        target[0:1, cols] = top
        target[1:2, cols] = total
        target[2:3, cols] = jnp.sum(delta, axis=0, keepdims=True) * total

    block(1)
    block(0)
    row = lax.broadcasted_iota(jnp.int32, (8, SEG), 0)
    after_stats[...] = jnp.where(row == 0, MASKED, 0.0)
    own_stats[3:8, :] = jnp.zeros((5, SEG), jnp.float32)
    count = rows_after(lengths_ref, segment)
    pl.when(count > 0)(lambda: block(2))
    pl.when(count > QB)(lambda: block(3))


def grads_kernel(
    lengths_ref,
    own_ref,
    before_ref,
    after_ref,
    own_stats,
    after_stats,
    own_there,
    after_there,
    own_out,
    before_out,
    after_out,
    k_win,
    v_win,
    q_win,
    d_win,
    dk_acc,
    dv_acc,
    dq_acc,
):
    segment, unused_slot = place()
    fill_windows(own_ref, before_ref, after_ref, k_win, v_win, q_win, d_win)
    bounds = doc_bounds(lengths_ref)
    base = (segment - 1) * SEG
    missing = segment == 0

    def block(qb):
        q_pos = segment * SEG + qb * QB + lax.broadcasted_iota(jnp.int32, (1, QB), 1)
        q_first = first_positions(bounds, q_pos)
        rows = slice(qb * QB, (qb + 1) * QB)
        q_rows = q_win[rows, :]
        d_rows = d_win[rows, :]
        cols = slice((qb % 2) * QB, (qb % 2 + 1) * QB)
        here = (own_stats if qb < 2 else after_stats)[:, cols]
        there = (own_there if qb < 2 else after_there)[:, cols]
        if qb < 2:
            row = lax.broadcasted_iota(jnp.int32, (8, QB), 0)
            there = jnp.where(missing, jnp.where(row == 0, MASKED, 0.0), there)
        top = jnp.maximum(here[0:1, :], there[0:1, :])
        here_share = jnp.exp2((here[0:1, :] - top) * EXPONENT)
        there_share = jnp.exp2((there[0:1, :] - top) * EXPONENT)
        total = here[1:2, :] * here_share + there[1:2, :] * there_share
        total = jnp.maximum(total, 1e-30)
        delta = (here[2:3, :] * here_share + there[2:3, :] * there_share) / total
        log_total = top * EXPONENT + jnp.log2(total)
        dq = jnp.zeros((QB, HD), jnp.float32)
        for kb in tiles_of(qb):
            keys = slice(kb * KB, (kb + 1) * KB)
            allowed = tile_allowed(base, q_pos, q_first, qb, kb)
            k_rows = k_win[keys, :]
            power = jnp.where(allowed, dot_t(k_rows, q_rows) * EXPONENT - log_total, MASKED)
            probs = jnp.exp2(power)
            d_probs = dot_t(v_win[keys, :], d_rows)
            d_scores = (probs * (d_probs - delta)).astype(jnp.bfloat16)
            dv = jnp.dot(probs.astype(jnp.bfloat16), d_rows, preferred_element_type=jnp.float32)
            dk = jnp.dot(d_scores, q_rows, preferred_element_type=jnp.float32)
            if qb == 1:
                dv_acc[keys, :] = dv
                dk_acc[keys, :] = dk
            else:
                dv_acc[keys, :] = dv_acc[keys, :] + dv
                dk_acc[keys, :] = dk_acc[keys, :] + dk
            dq = dq + lax.dot_general(
                d_scores, k_rows, CONTRACT_FIRST, preferred_element_type=jnp.float32
            )
        dq_acc[rows, :] = dq * SCALE

    dq_acc[SEG:WIN, :] = jnp.zeros((SEG, HD), jnp.float32)
    block(1)
    block(0)
    count = rows_after(lengths_ref, segment)
    pl.when(count > 0)(lambda: block(2))
    pl.when(count > QB)(lambda: block(3))

    for i in range(16):
        low = slice(i * ROWS, (i + 1) * ROWS)
        high = slice(SEG + i * ROWS, SEG + (i + 1) * ROWS)
        own_out[i, 0:ROWS, :] = dq_acc[low, :]
        own_out[i, ROWS : 2 * ROWS, :] = dk_acc[high, :] * SCALE
        own_out[i, 2 * ROWS : 3 * ROWS, :] = dv_acc[high, :]
        before_out[i, 0:ROWS, :] = (dk_acc[low, :] * SCALE).astype(jnp.bfloat16)
        before_out[i, ROWS : 2 * ROWS, :] = dv_acc[low, :].astype(jnp.bfloat16)
        after_out[i] = dq_acc[high, :].astype(jnp.bfloat16)


def merge_kernel(own_ref, dq_ref, dkv_ref, chunk_ref):
    for i in range(16):
        dq = own_ref[i, 0:ROWS, :] + dq_ref[i].astype(jnp.float32)
        dkv = own_ref[i, ROWS : 3 * ROWS, :] + dkv_ref[i].astype(jnp.float32)
        chunk_ref[i, 0:ROWS, :] = dq.astype(jnp.bfloat16)
        chunk_ref[i, ROWS : 3 * ROWS, :] = dkv.astype(jnp.bfloat16)


def finish_kernel(
    back_ref,
    key_prior_ref,
    value_prior_ref,
    dq_out,
    dk_out,
    dv_out,
    key_out,
    value_out,
):
    for h in range(HEADS):
        cols = slice(h * HD, (h + 1) * HD)
        dq_out[:, cols] = back_ref[h, 0:ROWS, :]
        dk = back_ref[h, ROWS : 2 * ROWS, :]
        dv = back_ref[h, 2 * ROWS : 3 * ROWS, :]
        dk_out[:, cols] = dk
        dv_out[:, cols] = dv
        dk = dk.astype(jnp.float32)
        dv = dv.astype(jnp.float32)
        key_out[:, cols] = key_prior_ref[:, cols] + dk * dk
        value_out[:, cols] = value_prior_ref[:, cols] + dv * dv


SMEM = pl.BlockSpec(memory_space=pltpu.SMEM)
VMEM = pl.BlockSpec(memory_space=pltpu.VMEM)


def bf16(*shape):
    return jax.ShapeDtypeStruct(shape, jnp.bfloat16)


HBM = pl.BlockSpec(memory_space=pltpu.HBM)


def call(kernel, inputs, outputs, specs, scratch=(), limit=16 << 20):
    return pl.pallas_call(
        kernel,
        in_specs=specs,
        out_specs=[VMEM] * len(outputs),
        out_shape=list(outputs),
        scratch_shapes=list(scratch),
        compiler_params=pltpu.CompilerParams(vmem_limit_bytes=limit),
        name=kernel.__name__,
    )(*inputs)


def shards(queries, keys, values, d_attn, fisher_key_prior, fisher_value_prior, doc_lengths):
    width = HEADS * HD
    half = bf16(16, 2 * ROWS, HD)
    (chunks,) = call(
        pack_kernel,
        (queries, keys, values, d_attn),
        (bf16(HEADS, 4 * ROWS, HD),),
        [HBM] * 4,
        scratch=[pltpu.VMEM((4, ROWS, width), jnp.bfloat16), pltpu.SemaphoreType.DMA((4,))],
        limit=60 << 20,
    )
    own = exchange(chunks)
    kv, qd = call(split_kernel, (own,), (half, half), [VMEM])
    kv_before = to_after(kv)
    qd_after = to_before(qd)
    windows = [pltpu.VMEM((WIN, HD), jnp.bfloat16)] * 4
    stats = jax.ShapeDtypeStruct((8, SEG), jnp.float32)
    own_stats, after_stats = call(
        stats_kernel,
        (doc_lengths, own, kv_before, qd_after),
        (stats, stats),
        [SMEM] + [VMEM] * 3,
        scratch=windows + [pltpu.VMEM((WIN, QB), jnp.float32)],
        limit=32 << 20,
    )
    own_there = to_after(after_stats)
    after_there = to_before(own_stats)
    own_grads, before_grads, after_grads = call(
        grads_kernel,
        (doc_lengths, own, kv_before, qd_after, own_stats, after_stats, own_there, after_there),
        (jax.ShapeDtypeStruct((16, 3 * ROWS, HD), jnp.float32), half, bf16(16, ROWS, HD)),
        [SMEM] + [VMEM] * 7,
        scratch=windows + [pltpu.VMEM((WIN, HD), jnp.float32)] * 3,
        limit=32 << 20,
    )
    dkv_there = to_before(before_grads)
    dq_there = to_after(after_grads)
    (merged,) = call(
        merge_kernel,
        (own_grads, dq_there, dkv_there),
        (bf16(16, 3 * ROWS, HD),),
        [VMEM] * 3,
    )
    back = exchange(merged)
    wide = jax.ShapeDtypeStruct((ROWS, width), jnp.float32)
    return call(
        finish_kernel,
        (back, fisher_key_prior, fisher_value_prior),
        (bf16(ROWS, width), bf16(ROWS, width), bf16(ROWS, width), wide, wide),
        [VMEM] * 3,
    )


def solution(mesh):
    tokens = P(AXES, None)
    return jax.shard_map(
        shards,
        mesh=mesh,
        in_specs=(tokens,) * 6 + (P(),),
        out_specs=(tokens,) * 5,
        check_vma=False,
    )
```

```python
import jax
import jax.numpy as jnp
from jax import lax
from jax.experimental import pallas as pl
from jax.experimental.pallas import tpu as pltpu
from jax.sharding import PartitionSpec as P

HD = 128
HEADS = 16
ROWS = 32
SEG = 512
SEGS = 32
NDOC = 32
TOKENS = SEG * SEGS
WIN = 2 * SEG
QB = 256
KB = 128
SCALE = 1.0 / HD**0.5
LOG2E = 1.4426950408889634
EXPONENT = SCALE * LOG2E
AXES = ("ctx", "head")
MASKED = -1e30


def device_of(segment, slot):
    column = slot % 4
    if segment < SEGS // 2:
        return (4 * segment + slot // 4) * 8 + column
    return (4 * (SEGS - 1 - segment) + 3 - slot // 4) * 8 + 4 + column


GROUPS = [[device_of(s, i) for i in range(16)] for s in range(SEGS)]
UP = [(device_of(s, i), device_of(s + 1, i)) for s in range(SEGS - 1) for i in range(16)]
DOWN = [(target, source) for source, target in UP]


def to_after(block):
    return lax.ppermute(block, AXES, UP)


def to_before(block):
    return lax.ppermute(block, AXES, DOWN)


def exchange(chunks):
    return lax.all_to_all(
        chunks, AXES, split_axis=0, concat_axis=0, axis_index_groups=GROUPS, tiled=True
    )


def place():
    ctx = lax.axis_index("ctx")
    head = lax.axis_index("head")
    lower = head < 4
    segment = jnp.where(lower, ctx // 4, SEGS - 1 - ctx // 4)
    slot = jnp.where(lower, ctx % 4, 3 - ctx % 4) * 4 + head % 4
    return segment.astype(jnp.int32), slot.astype(jnp.int32)


def doc_bounds(lengths_ref):
    bounds = []
    first = jnp.int32(0)
    for doc in range(NDOC):
        bounds.append(first)
        first = first + lengths_ref[doc]
    return bounds


def rows_after(lengths_ref, segment):
    start = segment * SEG
    count = jnp.int32(0)
    first = jnp.int32(0)
    for doc in range(NDOC):
        end = first + lengths_ref[doc]
        count = jnp.maximum(count, jnp.where(first < start, end - start - SEG, 0))
        first = end
    return count


def first_positions(bounds, q_pos):
    q_first = jnp.zeros(q_pos.shape, jnp.int32)
    for first in bounds:
        q_first = jnp.where(q_pos >= first, first, q_first)
    return jnp.where(q_pos >= TOKENS, TOKENS, q_first)


def tiles_of(qb):
    return range(6) if qb == 0 else range(8) if qb == 1 else range(4)


def own_tiles(qb):
    return range(4, 6) if qb == 0 else range(4, 8)


def rows_of(ref, first, count, part):
    rows = ref[first : first + count, part * ROWS : (part + 1) * ROWS, :]
    return rows.reshape(count * ROWS, HD)


def key_tile(own_ref, before_ref, kb, part):
    if kb < 4:
        return rows_of(before_ref, 4 * kb, 4, part)
    return rows_of(own_ref, 4 * (kb - 4), 4, part)


def query_block(own_ref, after_ref, qb, part):
    if qb < 2:
        return rows_of(own_ref, 8 * qb, 8, 2 + part)
    return rows_of(after_ref, 8 * (qb - 2), 8, part)


def positions(segment, qb):
    return segment * SEG + qb * QB + lax.broadcasted_iota(jnp.int32, (1, QB), 1)


def tile_allowed(base, q_pos, q_first, qb, kb):
    k_pos = base + kb * KB + lax.broadcasted_iota(jnp.int32, (KB, QB), 0)
    allowed = k_pos >= q_first
    if kb >= 4 + 2 * qb:
        allowed = allowed & (k_pos <= q_pos)
    return allowed


CONTRACT_LAST = (((1,), (1,)), ((), ()))
CONTRACT_FIRST = (((0,), (0,)), ((), ()))


def dot_t(left, right):
    return lax.dot_general(left, right, CONTRACT_LAST, preferred_element_type=jnp.float32)


def pack_kernel(q_hbm, k_hbm, v_hbm, d_hbm, chunk_ref, rows, sems):
    copies = [
        pltpu.make_async_copy(source, rows.at[part], sems.at[part])
        for part, source in enumerate((k_hbm, v_hbm, q_hbm, d_hbm))
    ]
    for copy in copies:
        copy.start()
    for part, copy in enumerate(copies):
        copy.wait()
        for h in range(HEADS):
            chunk_ref[h, part * ROWS : (part + 1) * ROWS, :] = rows[
                part, :, h * HD : (h + 1) * HD
            ]


def split_kernel(own_ref, kv_ref):
    for i in range(16):
        kv_ref[i] = own_ref[i, 0 : 2 * ROWS, :]


def block_stats(bounds, segment, qb, tiles, own_ref, before_ref, after_ref, s_buf):
    base = (segment - 1) * SEG
    q_pos = positions(segment, qb)
    q_first = first_positions(bounds, q_pos)
    q_rows = query_block(own_ref, after_ref, qb, 0)
    d_rows = query_block(own_ref, after_ref, qb, 1)
    top = jnp.full((8, QB), MASKED, jnp.float32)
    for kb in tiles:
        keys = slice(kb * KB, (kb + 1) * KB)
        allowed = tile_allowed(base, q_pos, q_first, qb, kb)
        k_rows = key_tile(own_ref, before_ref, kb, 0)
        scores = jnp.where(allowed, dot_t(k_rows, q_rows), MASKED)
        s_buf[keys, :] = scores
        top = jnp.maximum(top, jnp.max(scores.reshape(KB // 8, 8, QB), axis=0))
    top = jnp.max(top, axis=0, keepdims=True)
    total = jnp.zeros((8, QB), jnp.float32)
    for kb in tiles:
        keys = slice(kb * KB, (kb + 1) * KB)
        terms = jnp.exp2((s_buf[keys, :] - top) * EXPONENT)
        s_buf[keys, :] = terms
        total = total + jnp.sum(terms.reshape(KB // 8, 8, QB), axis=0)
    total = jnp.sum(total, axis=0, keepdims=True)
    inverse = 1.0 / total
    delta = jnp.zeros((8, QB), jnp.float32)
    for kb in tiles:
        keys = slice(kb * KB, (kb + 1) * KB)
        probs_b = (s_buf[keys, :] * inverse).astype(jnp.bfloat16).astype(jnp.float32)
        weighted = probs_b * dot_t(key_tile(own_ref, before_ref, kb, 1), d_rows)
        delta = delta + jnp.sum(weighted.reshape(KB // 8, 8, QB), axis=0)
    return top, total, jnp.sum(delta, axis=0, keepdims=True) * total


def down_kernel(lengths_ref, own_ref, qd_ref, s_buf, coded):
    segment, unused_slot = place()
    bounds = doc_bounds(lengths_ref)
    for i in range(16):
        qd_ref[i] = own_ref[i, 2 * ROWS : 4 * ROWS, :]
    coded[...] = jnp.zeros((2 * ROWS, HD), jnp.float32)
    for qb in range(2):
        stats = block_stats(bounds, segment, qb, own_tiles(qb), own_ref, None, None, s_buf)
        for number, rest in enumerate(stats):
            for piece in range(3):
                rounded = rest.astype(jnp.bfloat16).astype(jnp.float32)
                rest = rest - rounded
                for half in range(2):
                    row = (number * 3 + piece) * 4 + 2 * qb + half
                    coded[row : row + 1, :] = rounded[:, half * HD : (half + 1) * HD]
    qd_ref[16] = coded[...].astype(jnp.bfloat16)


def stats_kernel(
    lengths_ref, own_ref, before_ref, after_ref, own_stats, after_stats, s_buf, coded
):
    segment, unused_slot = place()
    bounds = doc_bounds(lengths_ref)
    for qb in (1, 0):
        stats = block_stats(bounds, segment, qb, tiles_of(qb), own_ref, before_ref, None, s_buf)
        for number in range(3):
            own_stats[number : number + 1, qb * QB : (qb + 1) * QB] = stats[number]
    own_stats[3:8, :] = jnp.zeros((5, SEG), jnp.float32)
    after_stats[...] = jnp.zeros((8, SEG), jnp.float32)

    def block(qb):
        here = block_stats(bounds, segment, qb, range(8), own_ref, before_ref, after_ref, s_buf)
        coded[...] = after_ref[16].astype(jnp.float32)
        there = []
        for number in range(3):
            halves = []
            for half in range(2):
                row = number * 12 + 2 * (qb - 2) + half
                halves.append(
                    coded[row : row + 1, :]
                    + coded[row + 4 : row + 5, :]
                    + coded[row + 8 : row + 9, :]
                )
            there.append(jnp.concatenate(halves, axis=1))
        top = jnp.maximum(here[0], there[0])
        here_share = jnp.exp2((here[0] - top) * EXPONENT)
        there_share = jnp.exp2((there[0] - top) * EXPONENT)
        cols = slice((qb - 2) * QB, (qb - 1) * QB)
        after_stats[0:1, cols] = top
        for number in (1, 2):
            after_stats[number : number + 1, cols] = (
                here[number] * here_share + there[number] * there_share
            )

    count = rows_after(lengths_ref, segment)
    pl.when(count > 0)(lambda: block(2))
    pl.when(count > QB)(lambda: block(3))


def grads_kernel(
    lengths_ref,
    own_ref,
    before_ref,
    after_ref,
    own_stats,
    after_stats,
    there_stats,
    own_out,
    before_out,
    after_out,
    dk_acc,
    dv_acc,
    dq_acc,
):
    segment, unused_slot = place()
    bounds = doc_bounds(lengths_ref)
    base = (segment - 1) * SEG
    from_before = rows_after(lengths_ref, segment - 1)

    def block(qb):
        q_pos = positions(segment, qb)
        q_first = first_positions(bounds, q_pos)
        q_rows = query_block(own_ref, after_ref, qb, 0)
        d_rows = query_block(own_ref, after_ref, qb, 1)
        cols = slice((qb % 2) * QB, (qb % 2 + 1) * QB)
        if qb < 2:
            whole = q_pos - segment * SEG >= from_before
            stats = [
                jnp.where(whole, own_stats[n : n + 1, cols], there_stats[n : n + 1, cols])
                for n in range(3)
            ]
        else:
            stats = [after_stats[n : n + 1, cols] for n in range(3)]
        top, total, delta = stats
        delta = delta / total
        log_total = top * EXPONENT + jnp.log2(total)
        dq = jnp.zeros((QB, HD), jnp.float32)
        for kb in tiles_of(qb):
            keys = slice(kb * KB, (kb + 1) * KB)
            allowed = tile_allowed(base, q_pos, q_first, qb, kb)
            k_rows = key_tile(own_ref, before_ref, kb, 0)
            power = jnp.where(allowed, dot_t(k_rows, q_rows) * EXPONENT - log_total, MASKED)
            probs = jnp.exp2(power)
            d_probs = dot_t(key_tile(own_ref, before_ref, kb, 1), d_rows)
            d_scores = (probs * (d_probs - delta)).astype(jnp.bfloat16)
            dv = jnp.dot(probs.astype(jnp.bfloat16), d_rows, preferred_element_type=jnp.float32)
            dk = jnp.dot(d_scores, q_rows, preferred_element_type=jnp.float32)
            if qb == 1:
                dv_acc[keys, :] = dv
                dk_acc[keys, :] = dk
            else:
                dv_acc[keys, :] = dv_acc[keys, :] + dv
                dk_acc[keys, :] = dk_acc[keys, :] + dk
            dq = dq + lax.dot_general(
                d_scores, k_rows, CONTRACT_FIRST, preferred_element_type=jnp.float32
            )
        dq_acc[qb * QB : (qb + 1) * QB, :] = dq * SCALE

    dq_acc[SEG:WIN, :] = jnp.zeros((SEG, HD), jnp.float32)
    block(1)
    block(0)
    count = rows_after(lengths_ref, segment)
    pl.when(count > 0)(lambda: block(2))
    pl.when(count > QB)(lambda: block(3))

    for i in range(16):
        low = slice(i * ROWS, (i + 1) * ROWS)
        high = slice(SEG + i * ROWS, SEG + (i + 1) * ROWS)
        own_out[i, 0:ROWS, :] = dq_acc[low, :]
        own_out[i, ROWS : 2 * ROWS, :] = dk_acc[high, :] * SCALE
        own_out[i, 2 * ROWS : 3 * ROWS, :] = dv_acc[high, :]
        before_out[i, 0:ROWS, :] = (dk_acc[low, :] * SCALE).astype(jnp.bfloat16)
        before_out[i, ROWS : 2 * ROWS, :] = dv_acc[low, :].astype(jnp.bfloat16)
        after_out[i] = dq_acc[high, :].astype(jnp.bfloat16)


def merge_kernel(own_ref, dq_ref, dkv_ref, chunk_ref):
    for i in range(16):
        dq = own_ref[i, 0:ROWS, :] + dq_ref[i].astype(jnp.float32)
        dkv = own_ref[i, ROWS : 3 * ROWS, :] + dkv_ref[i].astype(jnp.float32)
        chunk_ref[i, 0:ROWS, :] = dq.astype(jnp.bfloat16)
        chunk_ref[i, ROWS : 3 * ROWS, :] = dkv.astype(jnp.bfloat16)


def finish_kernel(
    back_ref,
    key_prior_ref,
    value_prior_ref,
    dq_out,
    dk_out,
    dv_out,
    key_out,
    value_out,
):
    for h in range(HEADS):
        cols = slice(h * HD, (h + 1) * HD)
        dq_out[:, cols] = back_ref[h, 0:ROWS, :]
        dk = back_ref[h, ROWS : 2 * ROWS, :]
        dv = back_ref[h, 2 * ROWS : 3 * ROWS, :]
        dk_out[:, cols] = dk
        dv_out[:, cols] = dv
        dk = dk.astype(jnp.float32)
        dv = dv.astype(jnp.float32)
        key_out[:, cols] = key_prior_ref[:, cols] + dk * dk
        value_out[:, cols] = value_prior_ref[:, cols] + dv * dv


SMEM = pl.BlockSpec(memory_space=pltpu.SMEM)
VMEM = pl.BlockSpec(memory_space=pltpu.VMEM)


def bf16(*shape):
    return jax.ShapeDtypeStruct(shape, jnp.bfloat16)


HBM = pl.BlockSpec(memory_space=pltpu.HBM)


def call(kernel, inputs, outputs, specs, scratch=(), limit=16 << 20):
    return pl.pallas_call(
        kernel,
        in_specs=specs,
        out_specs=[VMEM] * len(outputs),
        out_shape=list(outputs),
        scratch_shapes=list(scratch),
        compiler_params=pltpu.CompilerParams(vmem_limit_bytes=limit),
        name=kernel.__name__,
    )(*inputs)


def shards(queries, keys, values, d_attn, fisher_key_prior, fisher_value_prior, doc_lengths):
    width = HEADS * HD
    half = bf16(16, 2 * ROWS, HD)
    (chunks,) = call(
        pack_kernel,
        (queries, keys, values, d_attn),
        (bf16(HEADS, 4 * ROWS, HD),),
        [HBM] * 4,
        scratch=[pltpu.VMEM((4, ROWS, width), jnp.bfloat16), pltpu.SemaphoreType.DMA((4,))],
        limit=60 << 20,
    )
    own = exchange(chunks)
    (kv,) = call(split_kernel, (own,), (half,), [VMEM])
    kv_before = to_after(kv)
    scores = pltpu.VMEM((WIN, QB), jnp.float32)
    coded = pltpu.VMEM((2 * ROWS, HD), jnp.float32)
    (qd,) = call(
        down_kernel,
        (doc_lengths, own),
        (bf16(17, 2 * ROWS, HD),),
        [SMEM, VMEM],
        scratch=[scores, coded],
    )
    qd_after = to_before(qd)
    stats = jax.ShapeDtypeStruct((8, SEG), jnp.float32)
    own_stats, after_stats = call(
        stats_kernel,
        (doc_lengths, own, kv_before, qd_after),
        (stats, stats),
        [SMEM] + [VMEM] * 3,
        scratch=[scores, coded],
        limit=32 << 20,
    )
    there_stats = to_after(after_stats)
    own_grads, before_grads, after_grads = call(
        grads_kernel,
        (doc_lengths, own, kv_before, qd_after, own_stats, after_stats, there_stats),
        (jax.ShapeDtypeStruct((16, 3 * ROWS, HD), jnp.float32), half, bf16(16, ROWS, HD)),
        [SMEM] + [VMEM] * 6,
        scratch=[pltpu.VMEM((WIN, HD), jnp.float32)] * 3,
        limit=32 << 20,
    )
    dkv_there = to_before(before_grads)
    dq_there = to_after(after_grads)
    (merged,) = call(
        merge_kernel,
        (own_grads, dq_there, dkv_there),
        (bf16(16, 3 * ROWS, HD),),
        [VMEM] * 3,
    )
    back = exchange(merged)
    wide = jax.ShapeDtypeStruct((ROWS, width), jnp.float32)
    return call(
        finish_kernel,
        (back, fisher_key_prior, fisher_value_prior),
        (bf16(ROWS, width), bf16(ROWS, width), bf16(ROWS, width), wide, wide),
        [VMEM] * 3,
    )


def solution(mesh):
    tokens = P(AXES, None)
    return jax.shard_map(
        shards,
        mesh=mesh,
        in_specs=(tokens,) * 6 + (P(),),
        out_specs=(tokens,) * 5,
        check_vma=False,
    )
```

```python
import jax
import jax.numpy as jnp
from jax import lax
from jax.experimental import pallas as pl
from jax.experimental.pallas import tpu as pltpu
from jax.sharding import PartitionSpec as P

HD = 128
HEADS = 16
ROWS = 32
SEG = 512
SEGS = 32
NDOC = 32
TOKENS = SEG * SEGS
WIN = 2 * SEG
QB = 256
KB = 128
SCALE = 1.0 / HD**0.5
LOG2E = 1.4426950408889634
EXPONENT = SCALE * LOG2E
AXES = ("ctx", "head")
MASKED = -1e30


def device_of(segment, slot):
    column = slot % 4
    if segment < SEGS // 2:
        return (4 * segment + slot // 4) * 8 + column
    return (4 * (SEGS - 1 - segment) + 3 - slot // 4) * 8 + 4 + column


GROUPS = [[device_of(s, i) for i in range(16)] for s in range(SEGS)]
UP = [(device_of(s, i), device_of(s + 1, i)) for s in range(SEGS - 1) for i in range(16)]
DOWN = [(target, source) for source, target in UP]


def to_after(block):
    return lax.ppermute(block, AXES, UP)


def to_before(block):
    return lax.ppermute(block, AXES, DOWN)


def exchange(chunks):
    return lax.all_to_all(
        chunks, AXES, split_axis=0, concat_axis=0, axis_index_groups=GROUPS, tiled=True
    )


def place():
    ctx = lax.axis_index("ctx")
    head = lax.axis_index("head")
    lower = head < 4
    segment = jnp.where(lower, ctx // 4, SEGS - 1 - ctx // 4)
    slot = jnp.where(lower, ctx % 4, 3 - ctx % 4) * 4 + head % 4
    return segment.astype(jnp.int32), slot.astype(jnp.int32)


def rows_after(table, segment):
    start = segment * SEG
    count = jnp.int32(0)
    for first, end in table:
        count = jnp.maximum(count, jnp.where(first < start, end - start - SEG, 0))
    return count


def fill_info(lengths_ref, info_ref):
    segment, unused_slot = place()
    table = []
    first = jnp.int32(0)
    for doc in range(NDOC):
        end = first + lengths_ref[doc]
        table.append((first, end))
        first = end
    for part in range(2):
        q_pos = (segment + part) * SEG + lax.broadcasted_iota(jnp.int32, (1, SEG), 1)
        q_first = jnp.zeros((1, SEG), jnp.int32)
        for first, unused_end in table:
            q_first = jnp.where(q_pos >= first, first, q_first)
        q_first = jnp.where(q_pos >= TOKENS, TOKENS, q_first)
        info_ref[part : part + 1, :] = q_first - segment * SEG
        count = rows_after(table, segment - part)
        info_ref[2 + part : 3 + part, :] = jnp.full((1, SEG), count, jnp.int32)
    info_ref[4:8, :] = jnp.zeros((4, SEG), jnp.int32)


def info_scalar(info_ref, row):
    return jnp.max(info_ref[row : row + 1, 0:HD])


def tiles_of(qb):
    return range(6) if qb == 0 else range(8) if qb == 1 else range(4)


def own_tiles(qb):
    return range(4, 6) if qb == 0 else range(4, 8)


def rows_of(ref, first, count, part):
    rows = ref[first : first + count, part * ROWS : (part + 1) * ROWS, :]
    return rows.reshape(count * ROWS, HD)


def key_tile(own_ref, before_ref, kb, part):
    if kb < 4:
        return rows_of(before_ref, 4 * kb, 4, part)
    return rows_of(own_ref, 4 * (kb - 4), 4, part)


def query_block(own_ref, after_ref, qb, part):
    if qb < 2:
        return rows_of(own_ref, 8 * qb, 8, 2 + part)
    return rows_of(after_ref, 8 * (qb - 2), 8, part)


def tile_allowed(info_ref, qb, kb):
    q_first = info_ref[qb // 2 : qb // 2 + 1, (qb % 2) * QB : (qb % 2 + 1) * QB]
    k_pos = kb * KB - SEG + lax.broadcasted_iota(jnp.int32, (KB, QB), 0)
    allowed = k_pos >= q_first
    if kb >= 4 + 2 * qb:
        q_pos = qb * QB + lax.broadcasted_iota(jnp.int32, (1, QB), 1)
        allowed = allowed & (k_pos <= q_pos)
    return allowed


CONTRACT_LAST = (((1,), (1,)), ((), ()))
CONTRACT_FIRST = (((0,), (0,)), ((), ()))


def dot_t(left, right):
    return lax.dot_general(left, right, CONTRACT_LAST, preferred_element_type=jnp.float32)


def pack_kernel(q_hbm, k_hbm, v_hbm, d_hbm, chunk_ref, rows, sems):
    copies = [
        pltpu.make_async_copy(source, rows.at[part], sems.at[part])
        for part, source in enumerate((k_hbm, v_hbm, q_hbm, d_hbm))
    ]
    for copy in copies:
        copy.start()
    for part, copy in enumerate(copies):
        copy.wait()
        for h in range(HEADS):
            chunk_ref[h, part * ROWS : (part + 1) * ROWS, :] = rows[
                part, :, h * HD : (h + 1) * HD
            ]


def split_kernel(own_ref, kv_ref):
    for i in range(16):
        kv_ref[i] = own_ref[i, 0 : 2 * ROWS, :]


def block_stats(info_ref, qb, tiles, own_ref, before_ref, after_ref, s_buf):
    q_rows = query_block(own_ref, after_ref, qb, 0)
    d_rows = query_block(own_ref, after_ref, qb, 1)
    top = jnp.full((8, QB), MASKED, jnp.float32)
    for kb in tiles:
        keys = slice(kb * KB, (kb + 1) * KB)
        k_rows = key_tile(own_ref, before_ref, kb, 0)
        scores = jnp.where(tile_allowed(info_ref, qb, kb), dot_t(k_rows, q_rows), MASKED)
        s_buf[keys, :] = scores
        top = jnp.maximum(top, jnp.max(scores.reshape(KB // 8, 8, QB), axis=0))
    top = jnp.max(top, axis=0, keepdims=True)
    total = jnp.zeros((8, QB), jnp.float32)
    for kb in tiles:
        keys = slice(kb * KB, (kb + 1) * KB)
        terms = jnp.exp2((s_buf[keys, :] - top) * EXPONENT)
        s_buf[keys, :] = terms
        total = total + jnp.sum(terms.reshape(KB // 8, 8, QB), axis=0)
    total = jnp.sum(total, axis=0, keepdims=True)
    inverse = 1.0 / total
    delta = jnp.zeros((8, QB), jnp.float32)
    for kb in tiles:
        keys = slice(kb * KB, (kb + 1) * KB)
        probs_b = (s_buf[keys, :] * inverse).astype(jnp.bfloat16).astype(jnp.float32)
        weighted = probs_b * dot_t(key_tile(own_ref, before_ref, kb, 1), d_rows)
        delta = delta + jnp.sum(weighted.reshape(KB // 8, 8, QB), axis=0)
    return top, total, jnp.sum(delta, axis=0, keepdims=True) * total


def down_kernel(lengths_ref, own_ref, kv_ref, qd_ref, info_ref, s_buf, coded):
    for i in range(16):
        qd_ref[i] = own_ref[i, 2 * ROWS : 4 * ROWS, :]
    fill_info(lengths_ref, info_ref)
    coded[...] = jnp.zeros((2 * ROWS, HD), jnp.float32)
    for qb in range(2):
        stats = block_stats(info_ref, qb, own_tiles(qb), own_ref, None, None, s_buf)
        for number, rest in enumerate(stats):
            for piece in range(3):
                rounded = rest.astype(jnp.bfloat16).astype(jnp.float32)
                rest = rest - rounded
                for half in range(2):
                    row = (number * 3 + piece) * 4 + 2 * qb + half
                    coded[row : row + 1, :] = rounded[:, half * HD : (half + 1) * HD]
    qd_ref[16] = coded[...].astype(jnp.bfloat16)


def own_stats_kernel(info_ref, own_ref, before_ref, own_stats, s_buf):
    for qb in (1, 0):
        stats = block_stats(info_ref, qb, tiles_of(qb), own_ref, before_ref, None, s_buf)
        for number in range(3):
            own_stats[number : number + 1, qb * QB : (qb + 1) * QB] = stats[number]
    own_stats[3:8, :] = jnp.zeros((5, SEG), jnp.float32)


def after_stats_kernel(info_ref, own_ref, before_ref, after_ref, after_stats, s_buf, coded):
    after_stats[...] = jnp.zeros((8, SEG), jnp.float32)

    def block(qb):
        here = block_stats(info_ref, qb, range(8), own_ref, before_ref, after_ref, s_buf)
        there = []
        for number in range(3):
            halves = []
            for half in range(2):
                row = number * 12 + 2 * (qb - 2) + half
                halves.append(
                    coded[row : row + 1, :]
                    + coded[row + 4 : row + 5, :]
                    + coded[row + 8 : row + 9, :]
                )
            there.append(jnp.concatenate(halves, axis=1))
        top = jnp.maximum(here[0], there[0])
        here_share = jnp.exp2((here[0] - top) * EXPONENT)
        there_share = jnp.exp2((there[0] - top) * EXPONENT)
        cols = slice((qb - 2) * QB, (qb - 1) * QB)
        after_stats[0:1, cols] = top
        for number in (1, 2):
            after_stats[number : number + 1, cols] = (
                here[number] * here_share + there[number] * there_share
            )

    count = info_scalar(info_ref, 2)

    @pl.when(count > 0)
    def first_block():
        coded[...] = after_ref[16].astype(jnp.float32)
        block(2)

    pl.when(count > QB)(lambda: block(3))


def block_grads(
    info_ref, qb, stats, own_ref, before_ref, after_ref, dk_acc, dv_acc, dq_acc
):
    q_rows = query_block(own_ref, after_ref, qb, 0)
    d_rows = query_block(own_ref, after_ref, qb, 1)
    top, total, delta = stats
    delta = delta / total
    log_total = top * EXPONENT + jnp.log2(total)
    dq = jnp.zeros((HD, QB), jnp.float32)
    for kb in tiles_of(qb):
        keys = slice(kb * KB, (kb + 1) * KB)
        k_rows = key_tile(own_ref, before_ref, kb, 0)
        power = dot_t(k_rows, q_rows) * EXPONENT - log_total
        probs = jnp.exp2(jnp.where(tile_allowed(info_ref, qb, kb), power, MASKED))
        d_probs = dot_t(key_tile(own_ref, before_ref, kb, 1), d_rows)
        d_scores = (probs * (d_probs - delta)).astype(jnp.bfloat16)
        dv_acc[keys, :] = dv_acc[keys, :] + jnp.dot(
            probs.astype(jnp.bfloat16), d_rows, preferred_element_type=jnp.float32
        )
        dk_acc[keys, :] = dk_acc[keys, :] + jnp.dot(
            d_scores, q_rows, preferred_element_type=jnp.float32
        )
        dq = dq + lax.dot_general(
            k_rows, d_scores, CONTRACT_FIRST, preferred_element_type=jnp.float32
        )
    dq_acc[qb * QB : (qb + 1) * QB, :] = dq.T * SCALE


def early_kernel(
    info_ref, own_ref, before_ref, after_ref, own_stats, after_stats, dk_acc, dv_acc, dq_acc
):
    for acc in (dk_acc, dv_acc, dq_acc):
        acc[...] = jnp.zeros((WIN, HD), jnp.float32)

    def block(qb):
        cols = slice((qb % 2) * QB, (qb % 2 + 1) * QB)
        ref = own_stats if qb < 2 else after_stats
        stats = [ref[n : n + 1, cols] for n in range(3)]
        block_grads(
            info_ref, qb, stats, own_ref, before_ref, after_ref, dk_acc, dv_acc, dq_acc
        )

    from_before = info_scalar(info_ref, 3)
    count = info_scalar(info_ref, 2)
    pl.when(from_before <= QB)(lambda: block(1))
    pl.when(from_before <= 0)(lambda: block(0))
    pl.when(count > 0)(lambda: block(2))
    pl.when(count > QB)(lambda: block(3))


def late_kernel(
    info_ref,
    own_ref,
    before_ref,
    own_stats,
    there_stats,
    dk_in,
    dv_in,
    dq_in,
    own_out,
    before_out,
    after_out,
    dk_acc,
    dv_acc,
    dq_acc,
):
    dk_acc[...] = dk_in[...]
    dv_acc[...] = dv_in[...]
    dq_acc[...] = dq_in[...]

    def block(qb):
        cols = slice(qb * QB, (qb + 1) * QB)
        row = qb * QB + lax.broadcasted_iota(jnp.int32, (1, QB), 1)
        here = row >= info_ref[3:4, cols]
        stats = [
            jnp.where(here, own_stats[n : n + 1, cols], there_stats[n : n + 1, cols])
            for n in range(3)
        ]
        block_grads(info_ref, qb, stats, own_ref, before_ref, None, dk_acc, dv_acc, dq_acc)

    from_before = info_scalar(info_ref, 3)
    pl.when(from_before > QB)(lambda: block(1))
    pl.when(from_before > 0)(lambda: block(0))
    for i in range(16):
        low = slice(i * ROWS, (i + 1) * ROWS)
        high = slice(SEG + i * ROWS, SEG + (i + 1) * ROWS)
        own_out[i, 0:ROWS, :] = dq_acc[low, :]
        own_out[i, ROWS : 2 * ROWS, :] = dk_acc[high, :] * SCALE
        own_out[i, 2 * ROWS : 3 * ROWS, :] = dv_acc[high, :]
        before_out[i, 0:ROWS, :] = (dk_acc[low, :] * SCALE).astype(jnp.bfloat16)
        before_out[i, ROWS : 2 * ROWS, :] = dv_acc[low, :].astype(jnp.bfloat16)
        after_out[i] = dq_acc[high, :].astype(jnp.bfloat16)


def merge_kernel(own_ref, dq_ref, dkv_ref, chunk_ref):
    for i in range(16):
        dq = own_ref[i, 0:ROWS, :] + dq_ref[i].astype(jnp.float32)
        dkv = own_ref[i, ROWS : 3 * ROWS, :] + dkv_ref[i].astype(jnp.float32)
        chunk_ref[i, 0:ROWS, :] = dq.astype(jnp.bfloat16)
        chunk_ref[i, ROWS : 3 * ROWS, :] = dkv.astype(jnp.bfloat16)


def finish_kernel(
    back_ref,
    key_prior_ref,
    value_prior_ref,
    dq_out,
    dk_out,
    dv_out,
    key_out,
    value_out,
):
    for h in range(HEADS):
        cols = slice(h * HD, (h + 1) * HD)
        dq_out[:, cols] = back_ref[h, 0:ROWS, :]
        dk = back_ref[h, ROWS : 2 * ROWS, :]
        dv = back_ref[h, 2 * ROWS : 3 * ROWS, :]
        dk_out[:, cols] = dk
        dv_out[:, cols] = dv
        dk = dk.astype(jnp.float32)
        dv = dv.astype(jnp.float32)
        key_out[:, cols] = key_prior_ref[:, cols] + dk * dk
        value_out[:, cols] = value_prior_ref[:, cols] + dv * dv


SMEM = pl.BlockSpec(memory_space=pltpu.SMEM)
VMEM = pl.BlockSpec(memory_space=pltpu.VMEM)


def bf16(*shape):
    return jax.ShapeDtypeStruct(shape, jnp.bfloat16)


HBM = pl.BlockSpec(memory_space=pltpu.HBM)
ANY = pl.BlockSpec(memory_space=pl.ANY)


def call(
    kernel, inputs, outputs, specs, scratch=(), limit=16 << 20, gflop=0.5
):
    return pl.pallas_call(
        kernel,
        in_specs=specs,
        out_specs=[VMEM] * len(outputs),
        out_shape=list(outputs),
        scratch_shapes=list(scratch),
        cost_estimate=pl.CostEstimate(
            flops=int(gflop * 1e9), bytes_accessed=1 << 20, transcendentals=0
        ),
        compiler_params=pltpu.CompilerParams(vmem_limit_bytes=limit),
        name=kernel.__name__,
    )(*inputs)


def shards(queries, keys, values, d_attn, fisher_key_prior, fisher_value_prior, doc_lengths):
    width = HEADS * HD
    half = bf16(16, 2 * ROWS, HD)
    (chunks,) = call(
        pack_kernel,
        (queries, keys, values, d_attn),
        (bf16(HEADS, 4 * ROWS, HD),),
        [HBM] * 4,
        scratch=[pltpu.VMEM((4, ROWS, width), jnp.bfloat16), pltpu.SemaphoreType.DMA((4,))],
        limit=60 << 20,
    )
    own = exchange(chunks)
    (kv,) = call(split_kernel, (own,), (half,), [VMEM])
    kv_before = to_after(kv)
    scores = pltpu.VMEM((WIN, QB), jnp.float32)
    coded = pltpu.VMEM((2 * ROWS, HD), jnp.float32)
    qd, info = call(
        down_kernel,
        (doc_lengths, own, kv),
        (bf16(17, 2 * ROWS, HD), jax.ShapeDtypeStruct((8, SEG), jnp.int32)),
        [SMEM, VMEM, ANY],
        scratch=[scores, coded],
        gflop=1.0,
    )
    qd_after = to_before(qd)
    stats = jax.ShapeDtypeStruct((8, SEG), jnp.float32)
    (own_stats,) = call(
        own_stats_kernel,
        (info, own, kv_before),
        (stats,),
        [VMEM] * 3,
        scratch=[scores],
        gflop=1.5,
    )
    (after_stats,) = call(
        after_stats_kernel,
        (info, own, kv_before, qd_after),
        (stats,),
        [VMEM] * 4,
        scratch=[scores, coded],
        gflop=1.0,
    )
    there_stats = to_after(after_stats)
    acc = jax.ShapeDtypeStruct((WIN, HD), jnp.float32)
    sums = call(
        early_kernel,
        (info, own, kv_before, qd_after, own_stats, after_stats),
        (acc,) * 3,
        [VMEM] * 6,
        gflop=2.5,
    )
    own_grads, before_grads, after_grads = call(
        late_kernel,
        (info, own, kv_before, own_stats, there_stats, *sums),
        (
            jax.ShapeDtypeStruct((16, 3 * ROWS, HD), jnp.float32),
            half,
            bf16(16, ROWS, HD),
        ),
        [VMEM] * 8,
        scratch=[pltpu.VMEM((WIN, HD), jnp.float32)] * 3,
        gflop=2.0,
    )
    dkv_there = to_before(before_grads)
    dq_there = to_after(after_grads)
    (merged,) = call(
        merge_kernel,
        (own_grads, dq_there, dkv_there),
        (bf16(16, 3 * ROWS, HD),),
        [VMEM] * 3,
    )
    back = exchange(merged)
    wide = jax.ShapeDtypeStruct((ROWS, width), jnp.float32)
    return call(
        finish_kernel,
        (back, fisher_key_prior, fisher_value_prior),
        (bf16(ROWS, width), bf16(ROWS, width), bf16(ROWS, width), wide, wide),
        [VMEM] * 3,
    )


def solution(mesh):
    tokens = P(AXES, None)
    return jax.shard_map(
        shards,
        mesh=mesh,
        in_specs=(tokens,) * 6 + (P(),),
        out_specs=(tokens,) * 5,
        check_vma=False,
    )
```

```python
import jax
import jax.numpy as jnp
from jax import lax
from jax.experimental import pallas as pl
from jax.experimental.pallas import tpu as pltpu
from jax.sharding import PartitionSpec as P

HD = 128
HEADS = 16
ROWS = 32
SEG = 512
SEGS = 32
NDOC = 32
TOKENS = SEG * SEGS
WIN = 2 * SEG
QB = 256
KB = 128
SCALE = 1.0 / HD**0.5
LOG2E = 1.4426950408889634
EXPONENT = SCALE * LOG2E
AXES = ("ctx", "head")
MASKED = -1e30


def device_of(segment, slot):
    column = slot % 4
    if segment < SEGS // 2:
        return (4 * segment + slot // 4) * 8 + column
    return (4 * (SEGS - 1 - segment) + 3 - slot // 4) * 8 + 4 + column


GROUPS = [[device_of(s, i) for i in range(16)] for s in range(SEGS)]
UP = [(device_of(s, i), device_of(s + 1, i)) for s in range(SEGS - 1) for i in range(16)]
DOWN = [(target, source) for source, target in UP]


def to_after(block):
    return lax.ppermute(block, AXES, UP)


def to_before(block):
    return lax.ppermute(block, AXES, DOWN)


def exchange(chunks):
    return lax.all_to_all(
        chunks, AXES, split_axis=0, concat_axis=0, axis_index_groups=GROUPS, tiled=True
    )


def place():
    ctx = lax.axis_index("ctx")
    head = lax.axis_index("head")
    lower = head < 4
    segment = jnp.where(lower, ctx // 4, SEGS - 1 - ctx // 4)
    slot = jnp.where(lower, ctx % 4, 3 - ctx % 4) * 4 + head % 4
    return segment.astype(jnp.int32), slot.astype(jnp.int32)


def fill_info(lengths_ref, info_ref):
    segment, unused_slot = place()
    base = segment * SEG
    q_pos = base + lax.broadcasted_iota(jnp.int32, (1, 2 * SEG), 1)
    lengths = jnp.broadcast_to(lengths_ref[...].reshape(1, NDOC), (NDOC, NDOC))
    doc = lax.broadcasted_iota(jnp.int32, (NDOC, NDOC), 0)
    other = lax.broadcasted_iota(jnp.int32, (NDOC, NDOC), 1)
    starts = jnp.sum(jnp.where(other < doc, lengths, 0), axis=1, keepdims=True)
    q_first = jnp.max(jnp.where(starts <= q_pos, starts, 0), axis=0, keepdims=True)
    q_first = jnp.where(q_pos >= TOKENS, TOKENS, q_first) - base
    for part in range(2):
        firsts = q_first[:, part * SEG : (part + 1) * SEG]
        info_ref[part : part + 1, :] = firsts
        limit = -SEG if part == 0 else 0
        reach = jnp.sum((firsts < limit).astype(jnp.int32), axis=1, keepdims=True)
        info_ref[3 - part : 4 - part, :] = jnp.broadcast_to(reach, (1, SEG))
    info_ref[4:8, :] = jnp.zeros((4, SEG), jnp.int32)


def info_scalar(info_ref, row):
    return jnp.max(info_ref[row : row + 1, 0:HD])


def tiles_of(qb):
    return (range(6), range(8), range(4), range(2, 4))[qb]


def own_tiles(qb):
    return range(4, 6) if qb == 0 else range(4, 8)


def rows_of(ref, first, count, part):
    rows = ref[first : first + count, part * ROWS : (part + 1) * ROWS, :]
    return rows.reshape(count * ROWS, HD)


def key_tile(own_ref, before_ref, kb, part):
    if kb < 4:
        return rows_of(before_ref, 4 * kb, 4, part)
    return rows_of(own_ref, 4 * (kb - 4), 4, part)


def query_block(own_ref, after_ref, qb, part):
    if qb < 2:
        return rows_of(own_ref, 8 * qb, 8, 2 + part)
    return rows_of(after_ref, 8 * (qb - 2), 8, part)


def tile_allowed(info_ref, qb, kb):
    q_first = info_ref[qb // 2 : qb // 2 + 1, (qb % 2) * QB : (qb % 2 + 1) * QB]
    k_pos = kb * KB - SEG + lax.broadcasted_iota(jnp.int32, (KB, QB), 0)
    allowed = k_pos >= q_first
    if kb >= 4 + 2 * qb:
        q_pos = qb * QB + lax.broadcasted_iota(jnp.int32, (1, QB), 1)
        allowed = allowed & (k_pos <= q_pos)
    return allowed


CONTRACT_LAST = (((1,), (1,)), ((), ()))
CONTRACT_FIRST = (((0,), (0,)), ((), ()))


def dot_t(left, right):
    return lax.dot_general(left, right, CONTRACT_LAST, preferred_element_type=jnp.float32)


def pack_kernel(q_hbm, k_hbm, v_hbm, d_hbm, chunk_ref, rows, sems):
    copies = [
        pltpu.make_async_copy(source, rows.at[part], sems.at[part])
        for part, source in enumerate((k_hbm, v_hbm, q_hbm, d_hbm))
    ]
    for copy in copies:
        copy.start()
    for part, copy in enumerate(copies):
        copy.wait()
        for h in range(HEADS):
            chunk_ref[h, part * ROWS : (part + 1) * ROWS, :] = rows[
                part, :, h * HD : (h + 1) * HD
            ]


def split_kernel(own_ref, kv_ref):
    for i in range(16):
        kv_ref[i] = own_ref[i, 0 : 2 * ROWS, :]


def all_keys(own_ref, before_ref, tiles, part):
    return jnp.concatenate([key_tile(own_ref, before_ref, kb, part) for kb in tiles], axis=0)


def block_stats(info_ref, qb, tiles, own_ref, before_ref, after_ref, s_buf):
    q_rows = query_block(own_ref, after_ref, qb, 0)
    d_rows = query_block(own_ref, after_ref, qb, 1)
    top = jnp.full((8, QB), MASKED, jnp.float32)
    for kb in tiles:
        keys = slice(kb * KB, (kb + 1) * KB)
        k_rows = key_tile(own_ref, before_ref, kb, 0)
        scores = jnp.where(tile_allowed(info_ref, qb, kb), dot_t(k_rows, q_rows), MASKED)
        s_buf[keys, :] = scores
        top = jnp.maximum(top, jnp.max(scores.reshape(KB // 8, 8, QB), axis=0))
    top = jnp.max(top, axis=0, keepdims=True)
    total = jnp.zeros((8, QB), jnp.float32)
    for kb in tiles:
        keys = slice(kb * KB, (kb + 1) * KB)
        terms = jnp.exp2((s_buf[keys, :] - top) * EXPONENT)
        s_buf[keys, :] = terms
        total = total + jnp.sum(terms.reshape(KB // 8, 8, QB), axis=0)
    total = jnp.sum(total, axis=0, keepdims=True)
    inverse = 1.0 / total
    delta = jnp.zeros((8, QB), jnp.float32)
    for kb in tiles:
        keys = slice(kb * KB, (kb + 1) * KB)
        probs_b = (s_buf[keys, :] * inverse).astype(jnp.bfloat16).astype(jnp.float32)
        weighted = probs_b * dot_t(key_tile(own_ref, before_ref, kb, 1), d_rows)
        delta = delta + jnp.sum(weighted.reshape(KB // 8, 8, QB), axis=0)
    return top, total, jnp.sum(delta, axis=0, keepdims=True) * total


def down_kernel(lengths_ref, own_ref, kv_ref, qd_ref, info_ref, s_buf, coded):
    for i in range(16):
        qd_ref[i] = own_ref[i, 2 * ROWS : 4 * ROWS, :]
    fill_info(lengths_ref, info_ref)
    coded[...] = jnp.zeros((2 * ROWS, HD), jnp.float32)
    for qb in range(2):
        stats = block_stats(info_ref, qb, own_tiles(qb), own_ref, None, None, s_buf)
        for number, rest in enumerate(stats):
            for piece in range(3):
                rounded = rest.astype(jnp.bfloat16).astype(jnp.float32)
                rest = rest - rounded
                for half in range(2):
                    row = (number * 3 + piece) * 4 + 2 * qb + half
                    coded[row : row + 1, :] = rounded[:, half * HD : (half + 1) * HD]
    qd_ref[16] = coded[...].astype(jnp.bfloat16)


def own_stats_kernel(info_ref, own_ref, before_ref, own_stats, s_buf):
    for qb in (1, 0):
        stats = block_stats(info_ref, qb, tiles_of(qb), own_ref, before_ref, None, s_buf)
        for number in range(3):
            own_stats[number : number + 1, qb * QB : (qb + 1) * QB] = stats[number]
    own_stats[3:8, :] = jnp.zeros((5, SEG), jnp.float32)


def after_stats_kernel(info_ref, own_ref, before_ref, after_ref, after_stats, s_buf, coded):
    after_stats[...] = jnp.zeros((8, SEG), jnp.float32)

    def block(qb):
        here = block_stats(info_ref, qb, range(2 * qb - 4, 8), own_ref, before_ref, after_ref, s_buf)
        there = []
        for number in range(3):
            halves = []
            for half in range(2):
                row = number * 12 + 2 * (qb - 2) + half
                halves.append(
                    coded[row : row + 1, :]
                    + coded[row + 4 : row + 5, :]
                    + coded[row + 8 : row + 9, :]
                )
            there.append(jnp.concatenate(halves, axis=1))
        top = jnp.maximum(here[0], there[0])
        here_share = jnp.exp2((here[0] - top) * EXPONENT)
        there_share = jnp.exp2((there[0] - top) * EXPONENT)
        cols = slice((qb - 2) * QB, (qb - 1) * QB)
        after_stats[0:1, cols] = top
        for number in (1, 2):
            after_stats[number : number + 1, cols] = (
                here[number] * here_share + there[number] * there_share
            )

    count = info_scalar(info_ref, 2)

    @pl.when(count > 0)
    def first_block():
        coded[...] = after_ref[16].astype(jnp.float32)
        block(2)

    pl.when(count > QB)(lambda: block(3))


def block_grads(
    info_ref, qb, stats, own_ref, before_ref, after_ref, dk_acc, dv_acc, dq_acc, *bufs
):
    q_rows = query_block(own_ref, after_ref, qb, 0)
    d_rows = query_block(own_ref, after_ref, qb, 1)
    s_buf, dp_buf, p_buf, ds_buf = bufs
    top, total, delta = stats
    delta = delta / total
    log_total = top * EXPONENT + jnp.log2(total)
    tiles = tiles_of(qb)
    span = slice(tiles[0] * KB, (tiles[-1] + 1) * KB)
    k_rows = all_keys(own_ref, before_ref, tiles, 0)
    s_buf[span, :] = dot_t(k_rows, q_rows)
    dp_buf[span, :] = dot_t(all_keys(own_ref, before_ref, tiles, 1), d_rows)
    for kb in tiles:
        keys = slice(kb * KB, (kb + 1) * KB)
        power = s_buf[keys, :] * EXPONENT - log_total
        probs = jnp.exp2(jnp.where(tile_allowed(info_ref, qb, kb), power, MASKED))
        p_buf[keys, :] = probs.astype(jnp.bfloat16)
        ds_buf[keys, :] = (probs * (dp_buf[keys, :] - delta)).astype(jnp.bfloat16)
    d_scores = ds_buf[span, :]
    dv_acc[span, :] = dv_acc[span, :] + jnp.dot(
        p_buf[span, :], d_rows, preferred_element_type=jnp.float32
    )
    dk_acc[span, :] = dk_acc[span, :] + jnp.dot(
        d_scores, q_rows, preferred_element_type=jnp.float32
    )
    dq = lax.dot_general(k_rows, d_scores, CONTRACT_FIRST, preferred_element_type=jnp.float32)
    dq_acc[qb * QB : (qb + 1) * QB, :] = dq.T * SCALE


def own_block(info_ref, qb, stats, own_ref, before_ref, *refs):
    block_grads(info_ref, qb, stats, own_ref, before_ref, None, *refs)


def early_kernel(info_ref, own_ref, before_ref, own_stats, dk_acc, dv_acc, dq_acc, *bufs):
    dk_acc[...] = jnp.zeros((WIN, HD), jnp.float32)
    dv_acc[...] = jnp.zeros((WIN, HD), jnp.float32)

    def block(qb):
        stats = [own_stats[n : n + 1, qb * QB : (qb + 1) * QB] for n in range(3)]
        own_block(info_ref, qb, stats, own_ref, before_ref, dk_acc, dv_acc, dq_acc, *bufs)

    from_before = info_scalar(info_ref, 3)
    pl.when(from_before <= QB)(lambda: block(1))
    pl.when(from_before <= 0)(lambda: block(0))


def after_kernel(
    info_ref, before_ref, after_ref, after_stats, dk_acc, dv_acc, dq_out, dq_acc, *bufs
):
    dk_acc[...] = jnp.zeros((SEG, HD), jnp.float32)
    dv_acc[...] = jnp.zeros((SEG, HD), jnp.float32)
    dq_acc[...] = jnp.zeros((WIN, HD), jnp.float32)

    def block(qb):
        stats = [after_stats[n : n + 1, (qb - 2) * QB : (qb - 1) * QB] for n in range(3)]
        block_grads(
            info_ref, qb, stats, None, before_ref, after_ref, dk_acc, dv_acc, dq_acc, *bufs
        )

    count = info_scalar(info_ref, 2)
    pl.when(count > 0)(lambda: block(2))
    pl.when(count > QB)(lambda: block(3))
    for i in range(16):
        dq_out[i] = dq_acc[SEG + i * ROWS : SEG + (i + 1) * ROWS, :].astype(jnp.bfloat16)


def late_kernel(
    info_ref,
    own_ref,
    before_ref,
    own_stats,
    there_stats,
    dk_in,
    dv_in,
    dq_in,
    dk_after,
    dv_after,
    own_out,
    before_out,
    dk_acc,
    dv_acc,
    dq_acc,
    *bufs,
):
    dk_acc[0:SEG, :] = dk_in[0:SEG, :] + dk_after[...]
    dv_acc[0:SEG, :] = dv_in[0:SEG, :] + dv_after[...]
    dk_acc[SEG:WIN, :] = dk_in[SEG:WIN, :]
    dv_acc[SEG:WIN, :] = dv_in[SEG:WIN, :]
    dq_acc[...] = dq_in[...]

    def block(qb):
        cols = slice(qb * QB, (qb + 1) * QB)
        row = qb * QB + lax.broadcasted_iota(jnp.int32, (1, QB), 1)
        here = row >= info_ref[3:4, cols]
        stats = [
            jnp.where(here, own_stats[n : n + 1, cols], there_stats[n : n + 1, cols])
            for n in range(3)
        ]
        own_block(info_ref, qb, stats, own_ref, before_ref, dk_acc, dv_acc, dq_acc, *bufs)

    from_before = info_scalar(info_ref, 3)
    pl.when(from_before > QB)(lambda: block(1))
    pl.when(from_before > 0)(lambda: block(0))
    for i in range(16):
        low = slice(i * ROWS, (i + 1) * ROWS)
        high = slice(SEG + i * ROWS, SEG + (i + 1) * ROWS)
        own_out[i, 0:ROWS, :] = dq_acc[low, :]
        own_out[i, ROWS : 2 * ROWS, :] = dk_acc[high, :] * SCALE
        own_out[i, 2 * ROWS : 3 * ROWS, :] = dv_acc[high, :]
        before_out[i, 0:ROWS, :] = (dk_acc[low, :] * SCALE).astype(jnp.bfloat16)
        before_out[i, ROWS : 2 * ROWS, :] = dv_acc[low, :].astype(jnp.bfloat16)


def merge_kernel(own_ref, dq_ref, dkv_ref, chunk_ref):
    for i in range(16):
        dq = own_ref[i, 0:ROWS, :] + dq_ref[i].astype(jnp.float32)
        dkv = own_ref[i, ROWS : 3 * ROWS, :] + dkv_ref[i].astype(jnp.float32)
        chunk_ref[i, 0:ROWS, :] = dq.astype(jnp.bfloat16)
        chunk_ref[i, ROWS : 3 * ROWS, :] = dkv.astype(jnp.bfloat16)


def finish_kernel(
    back_ref,
    key_prior_ref,
    value_prior_ref,
    dq_out,
    dk_out,
    dv_out,
    key_out,
    value_out,
):
    for h in range(HEADS):
        cols = slice(h * HD, (h + 1) * HD)
        dq_out[:, cols] = back_ref[h, 0:ROWS, :]
        dk = back_ref[h, ROWS : 2 * ROWS, :]
        dv = back_ref[h, 2 * ROWS : 3 * ROWS, :]
        dk_out[:, cols] = dk
        dv_out[:, cols] = dv
        dk = dk.astype(jnp.float32)
        dv = dv.astype(jnp.float32)
        key_out[:, cols] = key_prior_ref[:, cols] + dk * dk
        value_out[:, cols] = value_prior_ref[:, cols] + dv * dv


SMEM = pl.BlockSpec(memory_space=pltpu.SMEM)
VMEM = pl.BlockSpec(memory_space=pltpu.VMEM)


def bf16(*shape):
    return jax.ShapeDtypeStruct(shape, jnp.bfloat16)


HBM = pl.BlockSpec(memory_space=pltpu.HBM)
ANY = pl.BlockSpec(memory_space=pl.ANY)


def call(
    kernel, inputs, outputs, specs, scratch=(), limit=16 << 20, gflop=0.5
):
    return pl.pallas_call(
        kernel,
        in_specs=specs,
        out_specs=[VMEM] * len(outputs),
        out_shape=list(outputs),
        scratch_shapes=list(scratch),
        cost_estimate=pl.CostEstimate(
            flops=int(gflop * 1e9), bytes_accessed=1 << 20, transcendentals=0
        ),
        compiler_params=pltpu.CompilerParams(vmem_limit_bytes=limit),
        name=kernel.__name__,
    )(*inputs)


def shards(queries, keys, values, d_attn, fisher_key_prior, fisher_value_prior, doc_lengths):
    width = HEADS * HD
    half = bf16(16, 2 * ROWS, HD)
    (chunks,) = call(
        pack_kernel,
        (queries, keys, values, d_attn),
        (bf16(HEADS, 4 * ROWS, HD),),
        [HBM] * 4,
        scratch=[pltpu.VMEM((4, ROWS, width), jnp.bfloat16), pltpu.SemaphoreType.DMA((4,))],
        limit=60 << 20,
    )
    own = exchange(chunks)
    (kv,) = call(split_kernel, (own,), (half,), [VMEM])
    kv_before = to_after(kv)
    scores = pltpu.VMEM((WIN, QB), jnp.float32)
    buffers = [scores] * 2 + [pltpu.VMEM((WIN, QB), jnp.bfloat16)] * 2
    coded = pltpu.VMEM((2 * ROWS, HD), jnp.float32)
    qd, info = call(
        down_kernel,
        (doc_lengths, own, kv),
        (bf16(17, 2 * ROWS, HD), jax.ShapeDtypeStruct((8, SEG), jnp.int32)),
        [VMEM, VMEM, ANY],
        scratch=[scores, coded],
        gflop=1.0,
    )
    qd_after = to_before(qd)
    stats = jax.ShapeDtypeStruct((8, SEG), jnp.float32)
    (own_stats,) = call(
        own_stats_kernel,
        (info, own, kv_before),
        (stats,),
        [VMEM] * 3,
        scratch=[scores],
        gflop=1.5,
    )
    (after_stats,) = call(
        after_stats_kernel,
        (info, own, kv_before, qd_after),
        (stats,),
        [VMEM] * 4,
        scratch=[scores, coded],
        gflop=1.0,
    )
    there_stats = to_after(after_stats)
    acc = jax.ShapeDtypeStruct((WIN, HD), jnp.float32)
    half_acc = jax.ShapeDtypeStruct((SEG, HD), jnp.float32)
    early = call(
        early_kernel,
        (info, own, kv_before, own_stats),
        (acc, acc, half_acc),
        [VMEM] * 4,
        scratch=buffers,
        gflop=2.5,
    )
    dk_after, dv_after, dq_after = call(
        after_kernel,
        (info, kv_before, qd_after, after_stats),
        (half_acc, half_acc, bf16(16, ROWS, HD)),
        [VMEM] * 4,
        scratch=[pltpu.VMEM((WIN, HD), jnp.float32)] + buffers,
        gflop=1.0,
    )
    own_grads, before_grads = call(
        late_kernel,
        (info, own, kv_before, own_stats, there_stats, *early, dk_after, dv_after),
        (jax.ShapeDtypeStruct((16, 3 * ROWS, HD), jnp.float32), half),
        [VMEM] * 10,
        scratch=[pltpu.VMEM((WIN, HD), jnp.float32)] * 2
        + [pltpu.VMEM((SEG, HD), jnp.float32)]
        + buffers,
        gflop=2.0,
    )
    dkv_there = to_before(before_grads)
    dq_there = to_after(dq_after)
    (merged,) = call(
        merge_kernel,
        (own_grads, dq_there, dkv_there),
        (bf16(16, 3 * ROWS, HD),),
        [VMEM] * 3,
    )
    back = exchange(merged)
    wide = jax.ShapeDtypeStruct((ROWS, width), jnp.float32)
    return call(
        finish_kernel,
        (back, fisher_key_prior, fisher_value_prior),
        (bf16(ROWS, width), bf16(ROWS, width), bf16(ROWS, width), wide, wide),
        [VMEM] * 3,
    )


def solution(mesh):
    tokens = P(AXES, None)
    return jax.shard_map(
        shards,
        mesh=mesh,
        in_specs=(tokens,) * 6 + (P(),),
        out_specs=(tokens,) * 5,
        check_vma=False,
    )
```

```python
import jax
import jax.numpy as jnp
from jax import lax
from jax.experimental import pallas as pl
from jax.experimental.pallas import tpu as pltpu
from jax.sharding import PartitionSpec as P

HD = 128
HEADS = 16
ROWS = 32
SEG = 512
SEGS = 32
NDOC = 32
TOKENS = SEG * SEGS
WIN = 2 * SEG
QB = 256
KB = 128
SCALE = 1.0 / HD**0.5
LOG2E = 1.4426950408889634
EXPONENT = SCALE * LOG2E
AXES = ("ctx", "head")
MASKED = -1e30


def device_of(segment, slot):
    column = slot % 4
    if segment < SEGS // 2:
        return (4 * segment + slot // 4) * 8 + column
    return (4 * (SEGS - 1 - segment) + 3 - slot // 4) * 8 + 4 + column


GROUPS = [[device_of(s, i) for i in range(16)] for s in range(SEGS)]
UP = [(device_of(s, i), device_of(s + 1, i)) for s in range(SEGS - 1) for i in range(16)]
DOWN = [(target, source) for source, target in UP]


def to_after(block):
    return lax.ppermute(block, AXES, UP)


def to_before(block):
    return lax.ppermute(block, AXES, DOWN)


def exchange(chunks):
    return lax.all_to_all(
        chunks, AXES, split_axis=0, concat_axis=0, axis_index_groups=GROUPS, tiled=True
    )


def place():
    ctx = lax.axis_index("ctx")
    head = lax.axis_index("head")
    lower = head < 4
    segment = jnp.where(lower, ctx // 4, SEGS - 1 - ctx // 4)
    slot = jnp.where(lower, ctx % 4, 3 - ctx % 4) * 4 + head % 4
    return segment.astype(jnp.int32), slot.astype(jnp.int32)


def fill_info(lengths_ref, info_ref):
    segment, unused_slot = place()
    base = segment * SEG
    q_pos = base + lax.broadcasted_iota(jnp.int32, (1, 2 * SEG), 1)
    lengths = jnp.broadcast_to(lengths_ref[...].reshape(1, NDOC), (NDOC, NDOC))
    doc = lax.broadcasted_iota(jnp.int32, (NDOC, NDOC), 0)
    other = lax.broadcasted_iota(jnp.int32, (NDOC, NDOC), 1)
    starts = jnp.sum(jnp.where(other < doc, lengths, 0), axis=1, keepdims=True)
    q_first = jnp.max(jnp.where(starts <= q_pos, starts, 0), axis=0, keepdims=True)
    q_first = jnp.where(q_pos >= TOKENS, TOKENS, q_first) - base
    for part in range(2):
        firsts = q_first[:, part * SEG : (part + 1) * SEG]
        info_ref[part : part + 1, :] = firsts
        limit = -SEG if part == 0 else 0
        reach = jnp.sum((firsts < limit).astype(jnp.int32), axis=1, keepdims=True)
        info_ref[3 - part : 4 - part, :] = jnp.broadcast_to(reach, (1, SEG))
    info_ref[4:8, :] = jnp.zeros((4, SEG), jnp.int32)


def info_scalar(info_ref, row):
    return jnp.max(info_ref[row : row + 1, 0:HD])


def tiles_of(qb):
    return (range(6), range(8), range(8), range(2, 8))[qb]


def own_tiles(qb):
    return range(4, 6) if qb == 0 else range(4, 8)


def rows_of(ref, first, count, part):
    rows = ref[first : first + count, part * ROWS : (part + 1) * ROWS, :]
    return rows.reshape(count * ROWS, HD)


def key_tile(own_ref, before_ref, kb, part):
    if kb < 4:
        return rows_of(before_ref, 4 * kb, 4, part)
    return rows_of(own_ref, 4 * (kb - 4), 4, part)


def query_block(own_ref, after_ref, qb, part):
    if qb < 2:
        return rows_of(own_ref, 8 * qb, 8, 2 + part)
    return rows_of(after_ref, 8 * (qb - 2), 8, part)


def row_firsts(info_ref, qb):
    return info_ref[qb // 2 : qb // 2 + 1, (qb % 2) * QB : (qb % 2 + 1) * QB]


def tile_allowed(q_first, qb, kb):
    k_pos = kb * KB - SEG + lax.broadcasted_iota(jnp.int32, (KB, QB), 0)
    allowed = k_pos >= q_first
    if kb >= 4 + 2 * qb:
        q_pos = qb * QB + lax.broadcasted_iota(jnp.int32, (1, QB), 1)
        allowed = allowed & (k_pos <= q_pos)
    return allowed


CONTRACT_LAST = (((1,), (1,)), ((), ()))
CONTRACT_FIRST = (((0,), (0,)), ((), ()))


def dot_t(left, right):
    return lax.dot_general(left, right, CONTRACT_LAST, preferred_element_type=jnp.float32)


def pack_kernel(q_hbm, k_hbm, v_hbm, d_hbm, chunk_ref, rows, sems):
    copies = [
        pltpu.make_async_copy(source, rows.at[part], sems.at[part])
        for part, source in enumerate((k_hbm, v_hbm, q_hbm, d_hbm))
    ]
    for copy in copies:
        copy.start()
    for part, copy in enumerate(copies):
        copy.wait()
        for h in range(HEADS):
            chunk_ref[h, part * ROWS : (part + 1) * ROWS, :] = rows[
                part, :, h * HD : (h + 1) * HD
            ]


def split_kernel(own_ref, kv_ref):
    for i in range(16):
        kv_ref[i] = own_ref[i, 0 : 2 * ROWS, :]


def all_keys(own_ref, before_ref, tiles, part):
    return jnp.concatenate([key_tile(own_ref, before_ref, kb, part) for kb in tiles], axis=0)


def block_stats(info_ref, qb, tiles, own_ref, before_ref, after_ref, s_buf):
    q_first = row_firsts(info_ref, qb)
    q_rows = query_block(own_ref, after_ref, qb, 0)
    d_rows = query_block(own_ref, after_ref, qb, 1)
    top = jnp.full((8, QB), MASKED, jnp.float32)
    for kb in tiles:
        keys = slice(kb * KB, (kb + 1) * KB)
        k_rows = key_tile(own_ref, before_ref, kb, 0)
        scores = jnp.where(tile_allowed(q_first, qb, kb), dot_t(k_rows, q_rows), MASKED)
        s_buf[keys, :] = scores
        top = jnp.maximum(top, jnp.max(scores.reshape(KB // 8, 8, QB), axis=0))
    top = jnp.max(top, axis=0, keepdims=True)
    total = jnp.zeros((8, QB), jnp.float32)
    for kb in tiles:
        keys = slice(kb * KB, (kb + 1) * KB)
        terms = jnp.exp2((s_buf[keys, :] - top) * EXPONENT)
        s_buf[keys, :] = terms
        total = total + jnp.sum(terms.reshape(KB // 8, 8, QB), axis=0)
    total = jnp.sum(total, axis=0, keepdims=True)
    inverse = 1.0 / total
    delta = jnp.zeros((8, QB), jnp.float32)
    for kb in tiles:
        keys = slice(kb * KB, (kb + 1) * KB)
        probs_b = (s_buf[keys, :] * inverse).astype(jnp.bfloat16).astype(jnp.float32)
        weighted = probs_b * dot_t(key_tile(own_ref, before_ref, kb, 1), d_rows)
        delta = delta + jnp.sum(weighted.reshape(KB // 8, 8, QB), axis=0)
    return top, total, jnp.sum(delta, axis=0, keepdims=True) * total


def encode(stats, half_block, coded):
    for number, rest in enumerate(stats):
        for piece in range(3):
            rounded = rest.astype(jnp.bfloat16).astype(jnp.float32)
            rest = rest - rounded
            for half in range(2):
                row = (number * 3 + piece) * 4 + 2 * half_block + half
                coded[row : row + 1, :] = rounded[:, half * HD : (half + 1) * HD]


def decode(half_block, coded):
    stats = []
    for number in range(3):
        halves = []
        for half in range(2):
            row = number * 12 + 2 * half_block + half
            halves.append(
                coded[row : row + 1, :] + coded[row + 4 : row + 5, :] + coded[row + 8 : row + 9, :]
            )
        stats.append(jnp.concatenate(halves, axis=1))
    return stats


def down_kernel(lengths_ref, own_ref, kv_ref, qd_ref, info_ref, s_buf, coded):
    for i in range(16):
        qd_ref[i] = own_ref[i, 2 * ROWS : 4 * ROWS, :]
    fill_info(lengths_ref, info_ref)
    coded[...] = jnp.zeros((2 * ROWS, HD), jnp.float32)
    for qb in range(2):
        stats = block_stats(info_ref, qb, own_tiles(qb), own_ref, None, None, s_buf)
        encode(stats, qb, coded)
    qd_ref[16] = coded[...].astype(jnp.bfloat16)


def own_stats_kernel(info_ref, own_ref, before_ref, own_stats, s_buf):
    for qb in (1, 0):
        stats = block_stats(info_ref, qb, tiles_of(qb), own_ref, before_ref, None, s_buf)
        for number in range(3):
            own_stats[number : number + 1, qb * QB : (qb + 1) * QB] = stats[number]
    own_stats[3:8, :] = jnp.zeros((5, SEG), jnp.float32)


def block_grads(
    q_first, qb, tiles, stats, own_ref, before_ref, after_ref, dk_acc, dv_acc, dq_acc, bufs
):
    q_rows = query_block(own_ref, after_ref, qb, 0)
    d_rows = query_block(own_ref, after_ref, qb, 1)
    s_buf, dp_buf, p_buf, ds_buf = bufs
    top, total, delta = stats
    delta = delta / total
    log_total = top * EXPONENT + jnp.log2(total)
    span = slice(tiles[0] * KB, (tiles[-1] + 1) * KB)
    k_rows = all_keys(own_ref, before_ref, tiles, 0)
    s_buf[span, :] = dot_t(k_rows, q_rows)
    dp_buf[span, :] = dot_t(all_keys(own_ref, before_ref, tiles, 1), d_rows)
    for kb in tiles:
        keys = slice(kb * KB, (kb + 1) * KB)
        power = s_buf[keys, :] * EXPONENT - log_total
        probs = jnp.exp2(jnp.where(tile_allowed(q_first, qb, kb), power, MASKED))
        p_buf[keys, :] = probs.astype(jnp.bfloat16)
        ds_buf[keys, :] = (probs * (dp_buf[keys, :] - delta)).astype(jnp.bfloat16)
    d_scores = ds_buf[span, :]
    dv_acc[span, :] = dv_acc[span, :] + jnp.dot(
        p_buf[span, :], d_rows, preferred_element_type=jnp.float32
    )
    dk_acc[span, :] = dk_acc[span, :] + jnp.dot(
        d_scores, q_rows, preferred_element_type=jnp.float32
    )
    dq = lax.dot_general(k_rows, d_scores, CONTRACT_FIRST, preferred_element_type=jnp.float32)
    rows = slice(qb * QB, (qb + 1) * QB)
    dq_acc[rows, :] = dq_acc[rows, :] + dq.T * SCALE


def early_kernel(info_ref, own_ref, before_ref, own_stats, dk_acc, dv_acc, dq_acc, *bufs):
    dk_acc[...] = jnp.zeros((WIN, HD), jnp.float32)
    dv_acc[...] = jnp.zeros((WIN, HD), jnp.float32)
    dq_acc[...] = jnp.zeros((SEG, HD), jnp.float32)
    for qb in (1, 0):
        q_first = row_firsts(info_ref, qb)
        q_first = jnp.where(q_first >= -SEG, q_first, WIN)
        stats = [own_stats[n : n + 1, qb * QB : (qb + 1) * QB] for n in range(3)]
        block_grads(
            q_first, qb, tiles_of(qb), stats, own_ref, before_ref, None, dk_acc, dv_acc, dq_acc, bufs
        )


def after_kernel(
    info_ref,
    own_ref,
    before_ref,
    after_ref,
    dk_in,
    dv_in,
    before_out,
    after_out,
    dk_out,
    dv_out,
    dk_acc,
    dv_acc,
    dq_acc,
    coded,
    *bufs,
):
    dk_acc[...] = dk_in[...]
    dv_acc[...] = dv_in[...]
    dq_acc[...] = jnp.zeros((WIN, HD), jnp.float32)

    def block(qb):
        tiles = tiles_of(qb)
        here = block_stats(info_ref, qb, tiles, own_ref, before_ref, after_ref, bufs[0])
        there = decode(qb - 2, coded)
        top = jnp.maximum(here[0], there[0])
        here_share = jnp.exp2((here[0] - top) * EXPONENT)
        there_share = jnp.exp2((there[0] - top) * EXPONENT)
        stats = [top] + [here[n] * here_share + there[n] * there_share for n in (1, 2)]
        encode(stats, qb - 2, coded)
        q_first = row_firsts(info_ref, qb)
        q_first = jnp.where(q_first < 0, q_first, WIN)
        block_grads(
            q_first, qb, tiles, stats, own_ref, before_ref, after_ref, dk_acc, dv_acc, dq_acc, bufs
        )

    coded[...] = after_ref[16].astype(jnp.float32)
    count = info_scalar(info_ref, 2)
    pl.when(count > 0)(lambda: block(2))
    pl.when(count > QB)(lambda: block(3))
    for i in range(16):
        low = slice(i * ROWS, (i + 1) * ROWS)
        before_out[i, 0:ROWS, :] = (dk_acc[low, :] * SCALE).astype(jnp.bfloat16)
        before_out[i, ROWS : 2 * ROWS, :] = dv_acc[low, :].astype(jnp.bfloat16)
        after_out[i] = dq_acc[SEG + i * ROWS : SEG + (i + 1) * ROWS, :].astype(jnp.bfloat16)
    for half in range(2):
        after_out[16 + half] = coded[half * ROWS : (half + 1) * ROWS, :].astype(jnp.bfloat16)
    dk_out[...] = dk_acc[SEG:WIN, :]
    dv_out[...] = dv_acc[SEG:WIN, :]


def late_kernel(
    info_ref,
    own_ref,
    dk_in,
    dv_in,
    dq_in,
    dq_there,
    dkv_there,
    chunk_ref,
    dk_acc,
    dv_acc,
    dq_acc,
    coded,
    *bufs,
):
    dk_acc[SEG:WIN, :] = dk_in[...]
    dv_acc[SEG:WIN, :] = dv_in[...]
    dq_acc[...] = dq_in[...]
    for half in range(2):
        coded[half * ROWS : (half + 1) * ROWS, :] = dq_there[16 + half].astype(jnp.float32)

    def block(qb):
        q_first = row_firsts(info_ref, qb)
        chosen = q_first < -SEG
        top, total, delta = decode(qb, coded)
        stats = (
            jnp.where(chosen, top, 0.0),
            jnp.where(chosen, total, 1.0),
            jnp.where(chosen, delta, 0.0),
        )
        q_first = jnp.where(chosen, q_first, WIN)
        block_grads(
            q_first, qb, own_tiles(qb), stats, own_ref, None, None, dk_acc, dv_acc, dq_acc, bufs
        )

    from_before = info_scalar(info_ref, 3)
    pl.when(from_before > 0)(lambda: block(0))
    pl.when(from_before > QB)(lambda: block(1))
    for i in range(16):
        low = slice(i * ROWS, (i + 1) * ROWS)
        high = slice(SEG + i * ROWS, SEG + (i + 1) * ROWS)
        dq = dq_acc[low, :] + dq_there[i].astype(jnp.float32)
        dk = dk_acc[high, :] * SCALE + dkv_there[i, 0:ROWS, :].astype(jnp.float32)
        dv = dv_acc[high, :] + dkv_there[i, ROWS : 2 * ROWS, :].astype(jnp.float32)
        for part, rows in enumerate((dq, dk, dv)):
            chunk_ref[i, part * ROWS : (part + 1) * ROWS, :] = rows.astype(jnp.bfloat16)


def finish_kernel(
    back_ref,
    key_prior_ref,
    value_prior_ref,
    dq_out,
    dk_out,
    dv_out,
    key_out,
    value_out,
):
    for h in range(HEADS):
        cols = slice(h * HD, (h + 1) * HD)
        dq_out[:, cols] = back_ref[h, 0:ROWS, :]
        dk = back_ref[h, ROWS : 2 * ROWS, :]
        dv = back_ref[h, 2 * ROWS : 3 * ROWS, :]
        dk_out[:, cols] = dk
        dv_out[:, cols] = dv
        dk = dk.astype(jnp.float32)
        dv = dv.astype(jnp.float32)
        key_out[:, cols] = key_prior_ref[:, cols] + dk * dk
        value_out[:, cols] = value_prior_ref[:, cols] + dv * dv


SMEM = pl.BlockSpec(memory_space=pltpu.SMEM)
VMEM = pl.BlockSpec(memory_space=pltpu.VMEM)


def bf16(*shape):
    return jax.ShapeDtypeStruct(shape, jnp.bfloat16)


HBM = pl.BlockSpec(memory_space=pltpu.HBM)
ANY = pl.BlockSpec(memory_space=pl.ANY)


def call(
    kernel, inputs, outputs, specs, scratch=(), limit=16 << 20, gflop=0.5
):
    return pl.pallas_call(
        kernel,
        in_specs=specs,
        out_specs=[VMEM] * len(outputs),
        out_shape=list(outputs),
        scratch_shapes=list(scratch),
        cost_estimate=pl.CostEstimate(
            flops=int(gflop * 1e9), bytes_accessed=1 << 20, transcendentals=0
        ),
        compiler_params=pltpu.CompilerParams(vmem_limit_bytes=limit),
        name=kernel.__name__,
    )(*inputs)


def shards(queries, keys, values, d_attn, fisher_key_prior, fisher_value_prior, doc_lengths):
    width = HEADS * HD
    half = bf16(16, 2 * ROWS, HD)
    (chunks,) = call(
        pack_kernel,
        (queries, keys, values, d_attn),
        (bf16(HEADS, 4 * ROWS, HD),),
        [HBM] * 4,
        scratch=[pltpu.VMEM((4, ROWS, width), jnp.bfloat16), pltpu.SemaphoreType.DMA((4,))],
        limit=60 << 20,
    )
    own = exchange(chunks)
    (kv,) = call(split_kernel, (own,), (half,), [VMEM])
    kv_before = to_after(kv)
    scores = pltpu.VMEM((WIN, QB), jnp.float32)
    buffers = [scores] * 2 + [pltpu.VMEM((WIN, QB), jnp.bfloat16)] * 2
    coded = pltpu.VMEM((2 * ROWS, HD), jnp.float32)
    qd, info = call(
        down_kernel,
        (doc_lengths, own, kv),
        (bf16(17, 2 * ROWS, HD), jax.ShapeDtypeStruct((8, SEG), jnp.int32)),
        [VMEM, VMEM, ANY],
        scratch=[scores, coded],
        gflop=1.0,
    )
    qd_after = to_before(qd)
    stats = jax.ShapeDtypeStruct((8, SEG), jnp.float32)
    (own_stats,) = call(
        own_stats_kernel,
        (info, own, kv_before),
        (stats,),
        [VMEM] * 3,
        scratch=[scores],
        gflop=1.5,
    )
    acc = jax.ShapeDtypeStruct((WIN, HD), jnp.float32)
    half_acc = jax.ShapeDtypeStruct((SEG, HD), jnp.float32)
    sums = pltpu.VMEM((WIN, HD), jnp.float32)
    dk_early, dv_early, dq_early = call(
        early_kernel,
        (info, own, kv_before, own_stats),
        (acc, acc, half_acc),
        [VMEM] * 4,
        scratch=buffers,
        gflop=2.0,
    )
    before_grads, after_grads, dk_own, dv_own = call(
        after_kernel,
        (info, own, kv_before, qd_after, dk_early, dv_early),
        (half, bf16(18, ROWS, HD), half_acc, half_acc),
        [VMEM] * 6,
        scratch=[sums, sums, sums, coded] + buffers,
        gflop=1.0,
    )
    dkv_there = to_before(before_grads)
    dq_there = to_after(after_grads)
    (merged,) = call(
        late_kernel,
        (info, own, dk_own, dv_own, dq_early, dq_there, dkv_there),
        (bf16(16, 3 * ROWS, HD),),
        [VMEM] * 7,
        scratch=[sums, sums, pltpu.VMEM((SEG, HD), jnp.float32), coded] + buffers,
    )
    back = exchange(merged)
    wide = jax.ShapeDtypeStruct((ROWS, width), jnp.float32)
    return call(
        finish_kernel,
        (back, fisher_key_prior, fisher_value_prior),
        (bf16(ROWS, width), bf16(ROWS, width), bf16(ROWS, width), wide, wide),
        [VMEM] * 3,
    )


def solution(mesh):
    tokens = P(AXES, None)
    return jax.shard_map(
        shards,
        mesh=mesh,
        in_specs=(tokens,) * 6 + (P(),),
        out_specs=(tokens,) * 5,
        check_vma=False,
    )
```

```python
import jax
import jax.numpy as jnp
from jax import lax
from jax.experimental import pallas as pl
from jax.experimental.pallas import tpu as pltpu
from jax.sharding import PartitionSpec as P

HD = 128
HEADS = 16
ROWS = 32
SEG = 512
SEGS = 32
NDOC = 32
TOKENS = SEG * SEGS
WIN = 2 * SEG
QB = 256
KB = 128
SCALE = 1.0 / HD**0.5
LOG2E = 1.4426950408889634
EXPONENT = SCALE * LOG2E
AXES = ("ctx", "head")
MASKED = -1e30


def device_of(segment, slot):
    column = slot % 4
    if segment < SEGS // 2:
        return (4 * segment + slot // 4) * 8 + column
    return (4 * (SEGS - 1 - segment) + 3 - slot // 4) * 8 + 4 + column


GROUPS = [[device_of(s, i) for i in range(16)] for s in range(SEGS)]
UP = [(device_of(s, i), device_of(s + 1, i)) for s in range(SEGS - 1) for i in range(16)]
EARLY = [(device_of(24, i), device_of(23, i)) for i in range(16)]
LATE = [(device_of(8, i), device_of(7, i)) for i in range(16)]
DOWN = [(target, source) for source, target in UP]
DOWN_REST = [pair for pair in DOWN if pair not in EARLY]
DOWN_FIRST = [pair for pair in DOWN if pair not in LATE]


def to_after(block):
    return lax.ppermute(block, AXES, UP)


def exchange(chunks):
    return lax.all_to_all(
        chunks, AXES, split_axis=0, concat_axis=0, axis_index_groups=GROUPS, tiled=True
    )


def place():
    ctx = lax.axis_index("ctx")
    head = lax.axis_index("head")
    lower = head < 4
    segment = jnp.where(lower, ctx // 4, SEGS - 1 - ctx // 4)
    slot = jnp.where(lower, ctx % 4, 3 - ctx % 4) * 4 + head % 4
    return segment.astype(jnp.int32), slot.astype(jnp.int32)


def fill_info(lengths_ref, info_ref):
    segment, unused_slot = place()
    base = segment * SEG
    q_pos = base + lax.broadcasted_iota(jnp.int32, (1, 2 * SEG), 1)
    lengths = jnp.broadcast_to(lengths_ref[...].reshape(1, NDOC), (NDOC, NDOC))
    doc = lax.broadcasted_iota(jnp.int32, (NDOC, NDOC), 0)
    other = lax.broadcasted_iota(jnp.int32, (NDOC, NDOC), 1)
    starts = jnp.sum(jnp.where(other < doc, lengths, 0), axis=1, keepdims=True)
    q_first = jnp.max(jnp.where(starts <= q_pos, starts, 0), axis=0, keepdims=True)
    q_first = jnp.where(q_pos >= TOKENS, TOKENS, q_first) - base
    for part in range(2):
        firsts = q_first[:, part * SEG : (part + 1) * SEG]
        info_ref[part : part + 1, :] = firsts
        limit = -SEG if part == 0 else 0
        reach = jnp.sum((firsts < limit).astype(jnp.int32), axis=1, keepdims=True)
        info_ref[3 - part : 4 - part, :] = jnp.broadcast_to(reach, (1, SEG))
    info_ref[4:8, :] = jnp.zeros((4, SEG), jnp.int32)


def info_scalar(info_ref, row):
    return jnp.max(info_ref[row : row + 1, 0:HD])


def tiles_of(qb):
    return (range(6), range(8), range(8), range(2, 8))[qb]


def own_tiles(qb):
    return range(4, 6) if qb == 0 else range(4, 8)


def rows_of(ref, first, count, part):
    rows = ref[first : first + count, part * ROWS : (part + 1) * ROWS, :]
    return rows.reshape(count * ROWS, HD)


def key_tile(own_ref, before_ref, kb, part):
    if kb < 4:
        return rows_of(before_ref, 4 * kb, 4, part)
    return rows_of(own_ref, 4 * (kb - 4), 4, part)


def query_block(own_ref, after_ref, qb, part):
    if qb < 2:
        return rows_of(own_ref, 8 * qb, 8, 2 + part)
    return rows_of(after_ref, 8 * (qb - 2), 8, part)


def row_firsts(info_ref, qb):
    return info_ref[qb // 2 : qb // 2 + 1, (qb % 2) * QB : (qb % 2 + 1) * QB]


def tile_allowed(q_first, qb, kb):
    k_pos = kb * KB - SEG + lax.broadcasted_iota(jnp.int32, (KB, QB), 0)
    allowed = k_pos >= q_first
    if kb >= 4 + 2 * qb:
        q_pos = qb * QB + lax.broadcasted_iota(jnp.int32, (1, QB), 1)
        allowed = allowed & (k_pos <= q_pos)
    return allowed


CONTRACT_LAST = (((1,), (1,)), ((), ()))
CONTRACT_FIRST = (((0,), (0,)), ((), ()))


def dot_t(left, right):
    return lax.dot_general(left, right, CONTRACT_LAST, preferred_element_type=jnp.float32)


def pack_kernel(q_hbm, k_hbm, v_hbm, d_hbm, chunk_ref, rows, sems):
    copies = [
        pltpu.make_async_copy(source, rows.at[part], sems.at[part])
        for part, source in enumerate((k_hbm, v_hbm, q_hbm, d_hbm))
    ]
    for copy in copies:
        copy.start()
    for part, copy in enumerate(copies):
        copy.wait()
        for h in range(HEADS):
            chunk_ref[h, part * ROWS : (part + 1) * ROWS, :] = rows[
                part, :, h * HD : (h + 1) * HD
            ]


def halves_kernel(pair_ref, first_ref, second_ref):
    for i in range(16):
        first_ref[i] = pair_ref[i, 0:ROWS, :]
        second_ref[i] = pair_ref[i, ROWS : 2 * ROWS, :]


def again_kernel(qd_ref, kv_ref, again_ref):
    again_ref[...] = qd_ref[...]


def split_kernel(own_ref, qd_ref, kv_ref):
    for i in range(16):
        kv_ref[i] = own_ref[i, 0 : 2 * ROWS, :]


def all_keys(own_ref, before_ref, tiles, part):
    return jnp.concatenate([key_tile(own_ref, before_ref, kb, part) for kb in tiles], axis=0)


def block_stats(info_ref, qb, tiles, own_ref, before_ref, after_ref, s_buf):
    q_first = row_firsts(info_ref, qb)
    q_rows = query_block(own_ref, after_ref, qb, 0)
    d_rows = query_block(own_ref, after_ref, qb, 1)
    top = jnp.full((8, QB), MASKED, jnp.float32)
    for kb in tiles:
        keys = slice(kb * KB, (kb + 1) * KB)
        k_rows = key_tile(own_ref, before_ref, kb, 0)
        scores = jnp.where(tile_allowed(q_first, qb, kb), dot_t(k_rows, q_rows), MASKED)
        s_buf[keys, :] = scores
        top = jnp.maximum(top, jnp.max(scores.reshape(KB // 8, 8, QB), axis=0))
    top = jnp.max(top, axis=0, keepdims=True)
    total = jnp.zeros((8, QB), jnp.float32)
    for kb in tiles:
        keys = slice(kb * KB, (kb + 1) * KB)
        terms = jnp.exp2((s_buf[keys, :] - top) * EXPONENT)
        s_buf[keys, :] = terms
        total = total + jnp.sum(terms.reshape(KB // 8, 8, QB), axis=0)
    total = jnp.sum(total, axis=0, keepdims=True)
    inverse = 1.0 / total
    delta = jnp.zeros((8, QB), jnp.float32)
    for kb in tiles:
        keys = slice(kb * KB, (kb + 1) * KB)
        probs_b = (s_buf[keys, :] * inverse).astype(jnp.bfloat16).astype(jnp.float32)
        weighted = probs_b * dot_t(key_tile(own_ref, before_ref, kb, 1), d_rows)
        delta = delta + jnp.sum(weighted.reshape(KB // 8, 8, QB), axis=0)
    return top, total, jnp.sum(delta, axis=0, keepdims=True) * total


def encode(stats, half_block, coded):
    for number, rest in enumerate(stats):
        for piece in range(3):
            rounded = rest.astype(jnp.bfloat16).astype(jnp.float32)
            rest = rest - rounded
            for half in range(2):
                row = (number * 3 + piece) * 4 + 2 * half_block + half
                coded[row : row + 1, :] = rounded[:, half * HD : (half + 1) * HD]


def decode(half_block, coded):
    stats = []
    for number in range(3):
        halves = []
        for half in range(2):
            row = number * 12 + 2 * half_block + half
            halves.append(
                coded[row : row + 1, :] + coded[row + 4 : row + 5, :] + coded[row + 8 : row + 9, :]
            )
        stats.append(jnp.concatenate(halves, axis=1))
    return stats


def down_kernel(lengths_ref, own_ref, qd_ref, info_ref, s_buf, coded):
    for i in range(16):
        qd_ref[i] = own_ref[i, 2 * ROWS : 4 * ROWS, :]
    fill_info(lengths_ref, info_ref)
    coded[...] = jnp.zeros((2 * ROWS, HD), jnp.float32)
    for qb in range(2):
        stats = block_stats(info_ref, qb, own_tiles(qb), own_ref, None, None, s_buf)
        encode(stats, qb, coded)
    qd_ref[16] = coded[...].astype(jnp.bfloat16)


def own_stats_kernel(info_ref, own_ref, before_ref, early_ref, own_stats, s_buf):
    for qb in (1, 0):
        stats = block_stats(info_ref, qb, tiles_of(qb), own_ref, before_ref, None, s_buf)
        for number in range(3):
            own_stats[number : number + 1, qb * QB : (qb + 1) * QB] = stats[number]
    own_stats[3:8, :] = jnp.zeros((5, SEG), jnp.float32)


def block_grads(
    q_first, qb, tiles, stats, own_ref, before_ref, after_ref, dk_acc, dv_acc, dq_acc, bufs
):
    q_rows = query_block(own_ref, after_ref, qb, 0)
    d_rows = query_block(own_ref, after_ref, qb, 1)
    s_buf, dp_buf, p_buf, ds_buf = bufs
    top, total, delta = stats
    delta = delta / total
    log_total = top * EXPONENT + jnp.log2(total)
    span = slice(tiles[0] * KB, (tiles[-1] + 1) * KB)
    k_rows = all_keys(own_ref, before_ref, tiles, 0)
    s_buf[span, :] = dot_t(k_rows, q_rows)
    dp_buf[span, :] = dot_t(all_keys(own_ref, before_ref, tiles, 1), d_rows)
    for kb in tiles:
        keys = slice(kb * KB, (kb + 1) * KB)
        power = s_buf[keys, :] * EXPONENT - log_total
        probs = jnp.exp2(jnp.where(tile_allowed(q_first, qb, kb), power, MASKED))
        p_buf[keys, :] = probs.astype(jnp.bfloat16)
        ds_buf[keys, :] = (probs * (dp_buf[keys, :] - delta)).astype(jnp.bfloat16)
    d_scores = ds_buf[span, :]
    dv_acc[span, :] = dv_acc[span, :] + jnp.dot(
        p_buf[span, :], d_rows, preferred_element_type=jnp.float32
    )
    dk_acc[span, :] = dk_acc[span, :] + jnp.dot(
        d_scores, q_rows, preferred_element_type=jnp.float32
    )
    dq = lax.dot_general(k_rows, d_scores, CONTRACT_FIRST, preferred_element_type=jnp.float32)
    rows = slice(qb * QB, (qb + 1) * QB)
    dq_acc[rows, :] = dq_acc[rows, :] + dq.T * SCALE


def early_kernel(info_ref, own_ref, before_ref, own_stats, dk_acc, dv_acc, dq_acc, *bufs):
    dk_acc[...] = jnp.zeros((WIN, HD), jnp.float32)
    dv_acc[...] = jnp.zeros((WIN, HD), jnp.float32)
    dq_acc[...] = jnp.zeros((SEG, HD), jnp.float32)
    for qb in (1, 0):
        q_first = row_firsts(info_ref, qb)
        q_first = jnp.where(q_first >= -SEG, q_first, WIN)
        stats = [own_stats[n : n + 1, qb * QB : (qb + 1) * QB] for n in range(3)]
        block_grads(
            q_first, qb, tiles_of(qb), stats, own_ref, before_ref, None, dk_acc, dv_acc, dq_acc, bufs
        )


def after_kernel(
    info_ref,
    own_ref,
    before_ref,
    rest_ref,
    early_ref,
    dk_in,
    dv_in,
    before_out,
    after_out,
    dk_out,
    dv_out,
    dk_acc,
    dv_acc,
    dq_acc,
    coded,
    after_ref,
    *bufs,
):
    dk_acc[...] = dk_in[...]
    dv_acc[...] = dv_in[...]
    dq_acc[...] = jnp.zeros((WIN, HD), jnp.float32)

    def block(qb):
        tiles = tiles_of(qb)
        here = block_stats(info_ref, qb, tiles, own_ref, before_ref, after_ref, bufs[0])
        there = decode(qb - 2, coded)
        top = jnp.maximum(here[0], there[0])
        here_share = jnp.exp2((here[0] - top) * EXPONENT)
        there_share = jnp.exp2((there[0] - top) * EXPONENT)
        stats = [top] + [here[n] * here_share + there[n] * there_share for n in (1, 2)]
        encode(stats, qb - 2, coded)
        q_first = row_firsts(info_ref, qb)
        q_first = jnp.where(q_first < 0, q_first, WIN)
        block_grads(
            q_first, qb, tiles, stats, own_ref, before_ref, after_ref, dk_acc, dv_acc, dq_acc, bufs
        )

    segment, unused_slot = place()

    @pl.when(segment == 23)
    def from_early():
        after_ref[...] = early_ref[...]

    @pl.when(segment != 23)
    def from_rest():
        after_ref[...] = rest_ref[...]

    coded[...] = after_ref[16].astype(jnp.float32)
    count = info_scalar(info_ref, 2)
    pl.when(count > 0)(lambda: block(2))
    pl.when(count > QB)(lambda: block(3))
    for i in range(16):
        low = slice(i * ROWS, (i + 1) * ROWS)
        before_out[i, 0:ROWS, :] = (dk_acc[low, :] * SCALE).astype(jnp.bfloat16)
        before_out[i, ROWS : 2 * ROWS, :] = dv_acc[low, :].astype(jnp.bfloat16)
        after_out[i] = dq_acc[SEG + i * ROWS : SEG + (i + 1) * ROWS, :].astype(jnp.bfloat16)
    for half in range(2):
        after_out[16 + half] = coded[half * ROWS : (half + 1) * ROWS, :].astype(jnp.bfloat16)
    dk_out[...] = dk_acc[SEG:WIN, :]
    dv_out[...] = dv_acc[SEG:WIN, :]


def late_kernel(
    info_ref,
    own_ref,
    dk_in,
    dv_in,
    dq_in,
    dq_there,
    dkv_first,
    dk_late,
    dv_late,
    chunk_ref,
    dk_acc,
    dv_acc,
    dq_acc,
    coded,
    *bufs,
):
    dk_acc[SEG:WIN, :] = dk_in[...]
    dv_acc[SEG:WIN, :] = dv_in[...]
    dq_acc[...] = dq_in[...]
    for half in range(2):
        coded[half * ROWS : (half + 1) * ROWS, :] = dq_there[16 + half].astype(jnp.float32)

    def block(qb):
        q_first = row_firsts(info_ref, qb)
        chosen = q_first < -SEG
        top, total, delta = decode(qb, coded)
        stats = (
            jnp.where(chosen, top, 0.0),
            jnp.where(chosen, total, 1.0),
            jnp.where(chosen, delta, 0.0),
        )
        q_first = jnp.where(chosen, q_first, WIN)
        block_grads(
            q_first, qb, own_tiles(qb), stats, own_ref, None, None, dk_acc, dv_acc, dq_acc, bufs
        )

    from_before = info_scalar(info_ref, 3)
    pl.when(from_before > 0)(lambda: block(0))
    pl.when(from_before > QB)(lambda: block(1))
    def finish(parts_of):
        for i in range(16):
            low = slice(i * ROWS, (i + 1) * ROWS)
            high = slice(SEG + i * ROWS, SEG + (i + 1) * ROWS)
            dq = dq_acc[low, :] + dq_there[i].astype(jnp.float32)
            dk = dk_acc[high, :] * SCALE + parts_of(i)[0].astype(jnp.float32)
            dv = dv_acc[high, :] + parts_of(i)[1].astype(jnp.float32)
            for part, rows in enumerate((dq, dk, dv)):
                chunk_ref[i, part * ROWS : (part + 1) * ROWS, :] = rows.astype(jnp.bfloat16)

    segment, unused_slot = place()

    @pl.when(segment == 7)
    def with_late():
        finish(lambda i: (dk_late[i], dv_late[i]))

    @pl.when(segment != 7)
    def with_first():
        finish(lambda i: (dkv_first[i, 0:ROWS, :], dkv_first[i, ROWS : 2 * ROWS, :]))


def finish_kernel(
    back_ref,
    key_prior_ref,
    value_prior_ref,
    dq_out,
    dk_out,
    dv_out,
    key_out,
    value_out,
):
    for h in range(HEADS):
        cols = slice(h * HD, (h + 1) * HD)
        dq_out[:, cols] = back_ref[h, 0:ROWS, :]
        dk = back_ref[h, ROWS : 2 * ROWS, :]
        dv = back_ref[h, 2 * ROWS : 3 * ROWS, :]
        dk_out[:, cols] = dk
        dv_out[:, cols] = dv
        dk = dk.astype(jnp.float32)
        dv = dv.astype(jnp.float32)
        key_out[:, cols] = key_prior_ref[:, cols] + dk * dk
        value_out[:, cols] = value_prior_ref[:, cols] + dv * dv


SMEM = pl.BlockSpec(memory_space=pltpu.SMEM)
VMEM = pl.BlockSpec(memory_space=pltpu.VMEM)


def bf16(*shape):
    return jax.ShapeDtypeStruct(shape, jnp.bfloat16)


HBM = pl.BlockSpec(memory_space=pltpu.HBM)
ANY = pl.BlockSpec(memory_space=pl.ANY)


def call(
    kernel, inputs, outputs, specs, scratch=(), limit=16 << 20, gflop=0.5
):
    return pl.pallas_call(
        kernel,
        in_specs=specs,
        out_specs=[VMEM] * len(outputs),
        out_shape=list(outputs),
        scratch_shapes=list(scratch),
        cost_estimate=pl.CostEstimate(
            flops=int(gflop * 1e9), bytes_accessed=1 << 20, transcendentals=0
        ),
        compiler_params=pltpu.CompilerParams(vmem_limit_bytes=limit),
        name=kernel.__name__,
    )(*inputs)


def shards(queries, keys, values, d_attn, fisher_key_prior, fisher_value_prior, doc_lengths):
    width = HEADS * HD
    half = bf16(16, 2 * ROWS, HD)
    (chunks,) = call(
        pack_kernel,
        (queries, keys, values, d_attn),
        (bf16(HEADS, 4 * ROWS, HD),),
        [HBM] * 4,
        scratch=[pltpu.VMEM((4, ROWS, width), jnp.bfloat16), pltpu.SemaphoreType.DMA((4,))],
        limit=60 << 20,
    )
    own = exchange(chunks)
    scores = pltpu.VMEM((WIN, QB), jnp.float32)
    buffers = [scores] * 2 + [pltpu.VMEM((WIN, QB), jnp.bfloat16)] * 2
    coded = pltpu.VMEM((2 * ROWS, HD), jnp.float32)
    pack = bf16(17, 2 * ROWS, HD)
    qd, info = call(
        down_kernel,
        (doc_lengths, own),
        (pack, jax.ShapeDtypeStruct((8, SEG), jnp.int32)),
        [VMEM, VMEM],
        scratch=[scores, coded],
        gflop=1.0,
    )
    qd_early = lax.ppermute(qd, AXES, EARLY)
    (kv,) = call(split_kernel, (own, qd), (half,), [VMEM, ANY])
    kv_before = to_after(kv)
    (qd_again,) = call(again_kernel, (qd, kv), (pack,), [VMEM, ANY])
    qd_rest = lax.ppermute(qd_again, AXES, DOWN_REST)
    stats = jax.ShapeDtypeStruct((8, SEG), jnp.float32)
    (own_stats,) = call(
        own_stats_kernel,
        (info, own, kv_before, qd_early),
        (stats,),
        [VMEM] * 3 + [ANY],
        scratch=[scores],
        gflop=1.5,
    )
    acc = jax.ShapeDtypeStruct((WIN, HD), jnp.float32)
    half_acc = jax.ShapeDtypeStruct((SEG, HD), jnp.float32)
    sums = pltpu.VMEM((WIN, HD), jnp.float32)
    dk_early, dv_early, dq_early = call(
        early_kernel,
        (info, own, kv_before, own_stats),
        (acc, acc, half_acc),
        [VMEM] * 4,
        scratch=buffers,
        gflop=2.0,
    )
    before_grads, after_grads, dk_own, dv_own = call(
        after_kernel,
        (info, own, kv_before, qd_rest, qd_early, dk_early, dv_early),
        (half, bf16(18, ROWS, HD), half_acc, half_acc),
        [VMEM] * 7,
        scratch=[sums, sums, sums, coded, pltpu.VMEM(pack.shape, pack.dtype)] + buffers,
        gflop=1.0,
    )
    dkv_first = lax.ppermute(before_grads, AXES, DOWN_FIRST)
    dq_there = to_after(after_grads)
    quarter = bf16(16, ROWS, HD)
    dk_late, dv_late = call(halves_kernel, (before_grads,), (quarter, quarter), [VMEM])
    dk_late = lax.ppermute(dk_late, AXES, LATE)
    dv_late = lax.ppermute(dv_late, AXES, LATE)
    (merged,) = call(
        late_kernel,
        (info, own, dk_own, dv_own, dq_early, dq_there, dkv_first, dk_late, dv_late),
        (bf16(16, 3 * ROWS, HD),),
        [VMEM] * 9,
        scratch=[sums, sums, pltpu.VMEM((SEG, HD), jnp.float32), coded] + buffers,
    )
    back = exchange(merged)
    wide = jax.ShapeDtypeStruct((ROWS, width), jnp.float32)
    return call(
        finish_kernel,
        (back, fisher_key_prior, fisher_value_prior),
        (bf16(ROWS, width), bf16(ROWS, width), bf16(ROWS, width), wide, wide),
        [VMEM] * 3,
    )


def solution(mesh):
    tokens = P(AXES, None)
    return jax.shard_map(
        shards,
        mesh=mesh,
        in_specs=(tokens,) * 6 + (P(),),
        out_specs=(tokens,) * 5,
        check_vma=False,
    )
```
